32 devices in a mesh: dp: 16 (over z, y, core), mp: 2 (over x).
Axes of the slice: x: 2, y: 2, z: 4, core: 2. Of those that a mesh axis runs over, the one named last changes fastest.
Arguments:
- inputs: bfloat16 [16384, 768], P(('dp', 'mp')), may hold values from -6 to 6
- norm_one: float32 [768], replicated, may hold values from 0.5 to 1.5
- w_query: bfloat16 [768, 768], P(None, 'mp'), may hold values from -0.3125 to 0.3125
- w_key: bfloat16 [768, 768], P(None, 'mp'), may hold values from -0.3125 to 0.3125
- w_value: bfloat16 [768, 768], P(None, 'mp'), may hold values from -0.21875 to 0.21875
- w_out: bfloat16 [768, 768], P('mp'), may hold values from -0.875 to 0.875
- bias_table: float32 [32, 12], P(None, 'mp'), may hold values from -4 to 4
- norm_two: float32 [768], replicated, may hold values from 0.5 to 1.5
- w_up: bfloat16 [768, 3072], P(None, 'mp'), may hold values from -0.21875 to 0.21875
- w_down: bfloat16 [3072, 768], P('mp'), may hold values from -0.15625 to 0.15625
- doc_lengths: int32 [16, 8], P('dp'), may hold values from 1 to 768, 1024 in all within a row
- layout_steps: int32 [16384], P('dp'), may hold values from 1 to 3
- cotangent: bfloat16 [16384, 768], P(('dp', 'mp')), may hold values from -6 to 6
Outputs:
- output: bfloat16 [16384, 768], P(('dp', 'mp'))
- input_grad: bfloat16 [16384, 768], P(('dp', 'mp'))
- grad_norm_one: float32 [768], replicated
- grad_norm_two: float32 [768], replicated
- grad_query: float32 [768, 768], P(None, 'mp')
- grad_key: float32 [768, 768], P(None, 'mp')
- grad_value: float32 [768, 768], P(None, 'mp')
- grad_out: float32 [768, 768], P('mp')
- grad_table: float32 [32, 12], P(None, 'mp')
- grad_up: float32 [768, 3072], P(None, 'mp')
- grad_down: float32 [3072, 768], P('mp')
The draws below stay inside these ranges and needn't reach their ends.
Inputs may be any that keep to these rules, and one draw needn't show every extreme that they name: `doc_lengths`: the 8 lengths of a row sum to 1024; the longest document of every row has exactly 768 tokens.
All inputs are finite; a program needn't handle non-finite values.
Results may differ from the reference program's by a relative error of at most 0.013.
Values may be sent and summed in bfloat16 or wider, within the bound.
No kernel may reach another device: no remote copies, remote signals or barrier semaphores. Data moves between devices by JAX's collectives and lax.ppermute only.
A program may use at most 192 MiB of HBM per device.

```python
import math
import jax
import jax.numpy as jnp
import numpy as np
from jax import lax

D = 768
H = 12
HD = 64
FF = 3072
BUCKETS = 32
MAX_DIST = 128
ROW_LEN = 1024
DOCS = 8
ROWS = 16
TOKENS = 16384


def place_ends(array, own_key, least, top_value):
    index_at = [jax.random.randint(jax.random.fold_in(own_key, axis), (), 0, length) for axis, length in enumerate(array.shape)]
    main_axis = array.shape.index(max(array.shape))
    next_to = index_at[:main_axis] + [(index_at[main_axis] + 1) % array.shape[main_axis]] + index_at[main_axis + 1:]
    return array.at[tuple(index_at)].set(least).at[tuple(next_to)].set(top_value)


def steps_of(rng, shape, shards, low, largest):
    loudness = 1.0
    for dim, blocks in shards:
        draws = jax.random.uniform(jax.random.fold_in(jax.random.fold_in(rng, 6), dim), (blocks,), jnp.float32, low / len(shards), largest / len(shards))
        loudness = loudness * jnp.repeat(jnp.exp(draws), shape[dim] // blocks).reshape((-1,) + (1,) * (len(shape) - 1 - dim))
    return loudness


def length_profile(count, total, bound, lean):
    weights = [(1 << 20) // math.isqrt(rank ** lean) + 1 for rank in range(2, count + 1)]
    surplus, given = total - bound - (count - 1), [1] * (count - 1)
    while surplus > 0:
        movable = [i for i in range(count - 1) if given[i] < bound]
        whole, left = sum([weights[i] for i in movable]), surplus
        for i in movable:
            more = min(bound - given[i], max(1, left * weights[i] // whole), surplus)
            given[i] = given[i] + more
            surplus = surplus - more
    return np.array([bound] + given)


def uneven_parts(key, count, total, bound, slope):
    if count == 2:
        one = jax.random.randint(key, (), max(1, total - bound), min(bound, total - 1) + 1)
        return jnp.stack([one, total - one])
    lengths = jnp.asarray(length_profile(count, total, bound, slope), jnp.int32)
    pairs = (count - 1) // 2
    giver, sink = lengths[1:1 + 2 * pairs:2], lengths[2:2 + 2 * pairs:2]
    margin = jnp.minimum(giver - 1, bound - sink)
    passed = jax.random.randint(jax.random.fold_in(key, 1), (pairs,), 0, 1 << 20) % (margin + 1)
    lengths = lengths.at[1:1 + 2 * pairs:2].set(giver - passed).at[2:2 + 2 * pairs:2].set(sink + passed)
    return lengths[jax.random.permutation(jax.random.fold_in(key, 2), count)]


def gaussian(stream_key, extent, scale, limit, cuts=(), kind=jnp.bfloat16):
    factor_of = steps_of(stream_key, extent, cuts, -0.22, 0.18) if cuts else 1.0
    array = jax.random.normal(stream_key, extent, jnp.float32) * scale * factor_of
    return jnp.minimum(jnp.maximum(array, -limit), limit).astype(kind)


def setup_inputs(seed: int = 0) -> dict:
    keys = jax.random.split(jax.random.key(seed), 14)
    inputs = gaussian(keys[0], (TOKENS, D), 1.0, 6.0, ((0, 32),))
    norm_one = jnp.clip(1.0 + 0.1 * jax.random.normal(keys[1], (D,), jnp.float32), 0.5, 1.5)
    w_query = gaussian(keys[2], (D, D), (D // 2) ** -0.5, 0.3125, ((1, 2),))
    w_key = gaussian(keys[3], (D, D), (D // 2) ** -0.5, 0.3125, ((1, 2),))
    w_value = gaussian(keys[4], (D, D), D ** -0.5, 0.21875, ((1, 2),))
    w_out = gaussian(keys[5], (D, D), (D // 16) ** -0.5, 0.875, ((0, 2),))
    bias_table = gaussian(keys[6], (BUCKETS, H), 1.0, 4.0, ((1, 2),), jnp.float32)
    norm_two = jnp.clip(1.0 + 0.1 * jax.random.normal(keys[7], (D,), jnp.float32), 0.5, 1.5)
    w_up = gaussian(keys[8], (D, FF), D ** -0.5, 0.21875, ((1, 2),))
    w_down = gaussian(keys[9], (FF, D), (FF // 2) ** -0.5, 0.15625, ((0, 2),))
    doc_lengths = jax.vmap(lambda own: uneven_parts(own, DOCS, ROW_LEN, 3 * ROW_LEN // 4, 2))(jax.random.split(keys[10], ROWS)).reshape((ROWS, DOCS)).astype(jnp.int32)
    layout_steps = place_ends(jax.random.randint(keys[11], (TOKENS,), 1, 4), jax.random.fold_in(keys[11], 1), 1, 3).astype(jnp.int32)
    cotangent = gaussian(keys[12], (TOKENS, D), 1.0, 6.0, ((0, 32),))
    return {"inputs": inputs, "norm_one": norm_one, "w_query": w_query, "w_key": w_key, "w_value": w_value, "w_out": w_out, "bias_table": bias_table, "norm_two": norm_two, "w_up": w_up, "w_down": w_down, "doc_lengths": doc_lengths, "layout_steps": layout_steps, "cotangent": cotangent}


EPS = 1e-06
MASKED = -1000000000.0
PRECISE = lax.Precision.HIGHEST

@jax.custom_vjp
def low(v):
    return lax.optimization_barrier(v.astype(jnp.bfloat16)).astype(jnp.float32)

@jax.custom_vjp
def low_back(v):
    return v

def low_keep(v):
    return (low(v), None)

def low_pass(kept, grad):
    return (grad,)

def back_keep(v):
    return (v, None)

def back_low(kept, grad):
    return (low(grad),)
low.defvjp(low_keep, low_pass)
low_back.defvjp(back_keep, back_low)

def bucket_limits(buckets, reach):
    halfway = buckets // 2
    exact_span = halfway // 2
    levels = halfway - exact_span
    limits = []
    for degree in range(1, levels):
        target = exact_span ** (levels - degree) * reach ** degree
        candidate = exact_span
        while candidate ** levels < target:
            candidate = candidate + 1
        limits.append(candidate)
    return limits

def relative_bucket(query_pos, key_pos):
    offset = key_pos[None, :] - query_pos[:, None]
    distance = jnp.abs(offset)
    halfway = BUCKETS // 2
    exact_span = halfway // 2
    bucket = jnp.where(offset > 0, halfway, 0) + jnp.minimum(distance, exact_span)
    for threshold in bucket_limits(BUCKETS, MAX_DIST):
        bucket = bucket + (distance >= threshold).astype(jnp.int32)
    return bucket.astype(jnp.int32)

def segments_of(doc_lengths, row_len):
    doc_ends = jnp.cumsum(doc_lengths, axis=1).astype(jnp.int32)
    places = jnp.arange(row_len, dtype=jnp.int32)
    return lax.optimization_barrier(jnp.sum((places[None, :, None] >= doc_ends[:, None, :]).astype(jnp.int32), axis=2)).astype(jnp.int32)

def rms_norm(values, scales):
    return values * lax.rsqrt(lax.optimization_barrier(jnp.mean(values * values, axis=-1, keepdims=True)) + EPS) * scales

def gelu_tanh(values):
    return jax.nn.gelu(values, approximate=True)

def matmul(left, right):
    return jnp.dot(left, right, preferred_element_type=jnp.float32, precision=PRECISE)

def row_attention(bias_table, queries, key_rows, value_rows, segment, position):
    same_doc = segment[:, None] == segment[None, :]
    bucket = relative_bucket(position, position)
    onehot = (bucket[:, :, None] == jnp.arange(BUCKETS, dtype=jnp.int32)[None, None, :]).astype(jnp.float32)
    rel_bias = jnp.einsum('qkb,bh->hqk', onehot, bias_table, precision=PRECISE)
    scores = jnp.einsum('qhd,khd->hqk', queries, key_rows, precision=PRECISE) * HD ** (-0.5) + rel_bias
    scores = low_back(scores)
    scores = jnp.where(same_doc[None], scores, MASKED)
    row_max = lax.optimization_barrier(jnp.max(scores, axis=-1, keepdims=True))
    exp_terms = jnp.exp(scores - row_max)
    soft_probs = exp_terms / lax.optimization_barrier(jnp.sum(exp_terms, axis=-1, keepdims=True))
    context = jnp.einsum('hqk,khd->qhd', low(soft_probs), value_rows, precision=PRECISE)
    return context.reshape(context.shape[0], -1)

def row_layer(weights_all, source, segment, position):
    norm_one, w_query, w_key, w_value, w_out, bias_table, norm_two, w_up, w_down = weights_all
    normed = low(rms_norm(source, norm_one))
    queries = low_back(low(matmul(normed, w_query)))
    key_rows = low_back(low(matmul(normed, w_key)))
    value_rows = low_back(low(matmul(normed, w_value)))
    head_shape = (source.shape[0], H, HD)
    context = low_back(low(row_attention(bias_table, queries.reshape(head_shape), key_rows.reshape(head_shape), value_rows.reshape(head_shape), segment, position)))
    attended = low_back(matmul(context, w_out))
    middle = source + attended
    normed_two = low(rms_norm(middle, norm_two))
    pre_act = low_back(matmul(normed_two, w_up))
    hidden = low(gelu_tanh(pre_act))
    lowered = low_back(matmul(hidden, w_down))
    return middle + lowered

def add_pair(earlier, later):
    return earlier + later

def reference(inputs, norm_one, w_query, w_key, w_value, w_out, bias_table, norm_two, w_up, w_down, doc_lengths, layout_steps, cotangent):
    weights_all = tuple((weight_arr.astype(jnp.float32) for weight_arr in (norm_one, w_query, w_key, w_value, w_out, bias_table, norm_two, w_up, w_down)))
    segment = segments_of(doc_lengths, ROW_LEN)
    position = jnp.cumsum(layout_steps.reshape(ROWS, ROW_LEN), axis=1).astype(jnp.int32)
    sources = inputs.astype(jnp.float32).reshape(ROWS, ROW_LEN, D)
    cotangents = cotangent.astype(jnp.float32).reshape(ROWS, ROW_LEN, D)

    def one_row(totals, pieces):
        source, row_cot, row_seg, row_pos = pieces

        def layer_of(params, values):
            return row_layer(params, values, row_seg, row_pos)
        result, pullback = jax.vjp(layer_of, weights_all, source)
        grad_params, grad_source = pullback(row_cot)
        totals = jax.tree.map(add_pair, totals, grad_params)
        return (totals, (result.astype(jnp.bfloat16), grad_source.astype(jnp.bfloat16)))
    zero_grads = jax.tree.map(jnp.zeros_like, weights_all)
    grads, (outputs, input_grads) = lax.scan(one_row, zero_grads, (sources, cotangents, segment, position))
    output = outputs.reshape(TOKENS, D)
    input_grad = input_grads.reshape(TOKENS, D)
    return (output, input_grad, grads[0], grads[6], grads[1], grads[2], grads[3], grads[4], grads[5], grads[7], grads[8])
```

```python
import functools

import jax
import jax.numpy as jnp
from jax import lax
from jax.experimental import pallas as pl
from jax.experimental.pallas import tpu as pltpu
from jax.sharding import PartitionSpec as P

HD = 64
BUCKETS = 32
MAX_DIST = 128
EPS = 1e-06
MASKED = -1000000000.0
BLK = 128
QB = 256
CUT = 64
GELU_C = 0.7978845608028654
GELU_A = 0.044715
BF = jnp.bfloat16
F32 = jnp.float32
VMEM_LIMIT = 56 * 1024 * 1024
SPARE = 4 * 1024 * 1024


def bucket_limits(buckets, reach):
    halfway = buckets // 2
    exact_span = halfway // 2
    levels = halfway - exact_span
    limits = []
    for degree in range(1, levels):
        target = exact_span ** (levels - degree) * reach**degree
        candidate = exact_span
        while candidate**levels < target:
            candidate = candidate + 1
        limits.append(candidate)
    return limits


LIMITS = bucket_limits(BUCKETS, MAX_DIST)


def dot(a, b):
    return jnp.dot(a, b, preferred_element_type=F32)


def dot_nt(a, b):
    return lax.dot_general(a, b, (((1,), (1,)), ((), ())), preferred_element_type=F32)


def band_blocks(long_blocks, blocks):
    steps = [n for n in range(blocks - 1) if n + 1 != long_blocks]
    return (
        [(n, n) for n in range(blocks)]
        + [(n + 1, n) for n in steps]
        + [(n, n + 1) for n in steps]
    )


def nbytes(shape, kind):
    if isinstance(kind, jax.ShapeDtypeStruct):
        kind = kind.dtype
    rows = -(-shape[-2] // 16) * 16 if len(shape) > 1 else 8
    lanes = -(-shape[-1] // BLK) * BLK
    lead = 1
    for n in shape[:-2]:
        lead = lead * n
    return lead * rows * lanes * jnp.dtype(kind).itemsize


def call(kernel, operands, outs, *, name, grid=(), scratch=(), after=(), limit=None):
    count = len(operands)

    def run(*refs):
        kernel(*refs[:count], *refs[count + len(after) :])

    arrays = list(operands) + list(outs)
    if not grid and any(
        s.block_shape is not None and tuple(s.block_shape) != v.shape for v, s in arrays
    ):
        grid = (1,)
    need = sum(nbytes(s.shape, s.dtype) for s in scratch if len(s.shape) > 1)
    for value, spec in arrays:
        if spec.block_shape is not None:
            need += (2 if grid else 1) * nbytes(spec.block_shape, value.dtype)
    limit = limit or min(VMEM_LIMIT, need + (need >> 3) + SPARE)
    return pl.pallas_call(
        run,
        grid=grid,
        in_specs=[spec for _, spec in operands]
        + [pl.BlockSpec(memory_space=pl.ANY)] * len(after),
        out_specs=[spec for _, spec in outs],
        out_shape=[kind for kind, _ in outs],
        scratch_shapes=list(scratch),
        compiler_params=pltpu.CompilerParams(
            vmem_limit_bytes=limit, dimension_semantics=("arbitrary",) * len(grid)
        ),
        cost_estimate=pl.CostEstimate(
            flops=1, bytes_accessed=1, transcendentals=0
        ),
        name=name,
    )(*[array for array, _ in operands], *after)


def full(shape):
    return pl.BlockSpec(shape, lambda *_: (0,) * len(shape))


def smem():
    return pl.BlockSpec(memory_space=pltpu.SMEM)


def put_rows(wide, row, value):
    total = wide.shape[1] // 2
    count = value.shape[0]
    for n in range(wide.shape[0]):
        cols = value[:, n * BLK : (n + 1) * BLK]
        wide[n, pl.ds(row, count), :] = cols
        wide[n, pl.ds(row + total, count), :] = cols


def get_rows(wide, row, count):
    return jnp.concatenate(
        [wide[n, pl.ds(row, count), :] for n in range(wide.shape[0])], axis=1
    )


def put_halves(wide, own_ref, oth_refs, mp):
    half = own_ref.shape[0]
    for side, refs in ((mp, [own_ref]), (1 - mp, oth_refs)):
        at = 0
        for ref in refs:
            for b in range(0, ref.shape[0], CUT):
                rows = ref[b : b + CUT, :].astype(F32)
                put_rows(wide, pl.multiple_of(side * half + at + b, CUT), rows)
            at += ref.shape[0]


def write_buckets(bkt_ref, posc, posr, segc, segr, band, long_blocks):
    for n, (j, i) in enumerate(band):
        rows, cols = slice(j * BLK, (j + 1) * BLK), slice(i * BLK, (i + 1) * BLK)
        offset = posc[rows, :] - posr[:, cols]
        distance = jnp.abs(offset)
        bucket = jnp.where(offset > 0, BUCKETS // 2, 0) + jnp.minimum(
            distance, BUCKETS // 4
        )
        for limit in LIMITS:
            bucket = bucket + jnp.where(distance >= limit, 1, 0)
        if j >= long_blocks:
            bucket = jnp.where(segc[rows, :] == segr[:, cols], bucket, BUCKETS)
        bkt_ref[n] = bucket


def attend_pair(p, qs, k, v_t, tab_ref, bkt_ref, p_long, p_tail, work, band):
    scores, values, queries, k_ref, ctx_t, inv_t = work
    long, total = p_long.shape[1], ctx_t.shape[1]
    index = {pair: n for n, pair in enumerate(band)}
    lane = lax.broadcasted_iota(jnp.int32, (total, 2 * HD), 1)
    k_ref[...] = k
    tables = []
    for hh in range(2):
        values[hh, 0:HD, :] = v_t[hh * HD : (hh + 1) * HD, :]
        values[hh, HD:, :] = jnp.ones((values.shape[1] - HD, total), BF)
        queries[hh] = jnp.where((lane < HD) == (hh == 0), qs, jnp.zeros_like(qs))
        row = tab_ref[pl.ds(2 * p + hh, 1), :]
        tables.append(
            (
                jnp.broadcast_to(row, (BLK, BLK)),
                row[:, BUCKETS // 2 - 1 : BUCKETS // 2],
                row[:, BUCKETS - 1 : BUCKETS],
            )
        )
    units = [(hh, start) for hh in range(2) for start in range(0, total, QB)]
    tops = {}

    def span(u):
        return (0, long) if units[u][1] < long else (long, total)

    def score(u, j):
        hh, start = units[u]
        lo = span(u)[0]
        table, behind, ahead = tables[hh]
        cells = dot_nt(k_ref[j : j + BLK, :], queries[hh, start : start + QB, :])
        tops_here = []
        for c in range(0, QB, BLK):
            pair = (j // BLK, (start + c) // BLK)
            if pair in index:
                bias = jnp.take_along_axis(
                    table, bkt_ref[index[pair]], axis=1, mode="promise_in_bounds"
                )
            else:
                bias = ahead if pair[0] > pair[1] else behind
            cell = cells[:, c : c + BLK] + bias
            scores[u % 2, j - lo : j - lo + BLK, c : c + BLK] = cell
            tops_here.append(jnp.max(cell.reshape(BLK // 8, 8, BLK), axis=0))
        top = jnp.concatenate(tops_here, axis=1)
        tops[u] = jnp.maximum(tops[u], top) if u in tops else top

    def term(u, j):
        hh, start = units[u]
        lo = span(u)[0]
        out = p_long if start < long else p_tail
        if j == lo:
            tops[u] = jnp.max(tops[u], axis=0, keepdims=True)
        terms = jnp.exp(scores[u % 2, j - lo : j - lo + BLK, :] - tops[u])
        out[hh, j - lo : j - lo + BLK, start - lo : start - lo + QB] = terms.astype(BF)

    def context(u):
        hh, start = units[u]
        lo, hi = span(u)
        out = p_long if start < long else p_tail
        sums = dot(values[hh, :, lo:hi], out[hh, :, start - lo : start - lo + QB])
        inverse = 1.0 / sums[HD : HD + 1, :]
        rows, cols = slice(hh * HD, (hh + 1) * HD), slice(start, start + QB)
        ctx_t[rows, cols] = sums[0:HD, :] * inverse
        if inv_t is not None:
            inv_t[rows, cols] = jnp.broadcast_to(inverse, (HD, QB))

    for j in range(*span(0), BLK):
        score(0, j)
    for u in range(len(units)):
        ahead_of = list(range(*span(u + 1), BLK)) if u + 1 < len(units) else []
        here = list(range(*span(u), BLK))
        for n in range(max(len(ahead_of), len(here))):
            if n < len(ahead_of):
                score(u + 1, ahead_of[n])
            if n < len(here):
                term(u, here[n])
        context(u)


def pieces_kernel(at, wo, up, down, cot, ffn_ref, out_ref, cot_ref, sems):
    rows, width = ffn_ref.shape[0], down.shape[1]
    part = out_ref.shape[1]
    start = pl.multiple_of(at[0] * rows, 16)
    first = pltpu.make_async_copy(
        wo.at[:, pl.ds(pl.multiple_of(at[1] * part, BLK), part)], out_ref, sems.at[0]
    )
    first.start()
    rows_of_cot = pltpu.make_async_copy(
        cot.at[0 : cot_ref.shape[0], :], cot_ref, sems.at[3]
    )
    rows_of_cot.start()

    @pl.when(at[1] == 0)
    def _():
        copy = pltpu.make_async_copy(up.at[pl.ds(start, rows), :], ffn_ref, sems.at[1])
        copy.start()
        copy.wait()

    @pl.when(at[1] == 1)
    def _():
        copies = [
            pltpu.make_async_copy(
                down.at[pl.ds(n * width + start, rows), :],
                ffn_ref.at[:, n * width : (n + 1) * width],
                sems.at[1 + n],
            )
            for n in range(2)
        ]
        for copy in copies:
            copy.start()
        for copy in copies:
            copy.wait()

    first.wait()
    rows_of_cot.wait()


def copy_kernel(*refs):
    for x_ref, out_ref in zip(refs[: len(refs) // 2], refs[len(refs) // 2 :]):
        out_ref[...] = x_ref[...]


def attn_own_kernel(
    long, band,
    meta, x_own, x_oth, gain, place_ref, wq, wk, wv, tab,
    xr_ref, nx_ref, q_ref, k_ref, v_ref, ctx_ref, inv_ref, pl_ref, pt_ref, bkt_ref,
    wide, scores, vals, queries, keys, ctx_t, inv_t,
):
    p = pl.program_id(0)
    total = xr_ref.shape[0]

    @pl.when(p == 0)
    def _():
        put_halves(wide, x_own, [x_oth], meta[1])
        for b in range(0, total, QB):
            rows = get_rows(wide, meta[0] + b, QB)
            xr_ref[b : b + QB, :] = rows.astype(BF)
            scale = lax.rsqrt(jnp.mean(rows * rows, axis=-1, keepdims=True) + EPS)
            nx_ref[b : b + QB, :] = (rows * scale * gain[...]).astype(BF)
        places = place_ref[...].astype(F32)
        down = [
            jnp.broadcast_to(places[n : n + 1, :], (BLK, total)).T.astype(jnp.int32)
            for n in range(2)
        ]
        write_buckets(
            bkt_ref, down[0], place_ref[0:1, :], down[1], place_ref[1:2, :], band,
            long // BLK,
        )

    nx = nx_ref[...]
    qs = (dot(nx, wq[...]).astype(BF).astype(F32) * HD ** (-0.5)).astype(BF)
    k = dot(nx, wk[...]).astype(BF)
    v = dot(nx, wv[...]).astype(BF)
    q_ref[...] = qs
    k_ref[...] = k
    v_ref[...] = v
    work = (scores, vals, queries, keys, ctx_t, inv_t)
    attend_pair(p, qs, k, v.T, tab, bkt_ref, pl_ref, pt_ref, work, band)
    ctx_ref[...] = ctx_t[...].T.astype(BF)
    inv_ref[...] = inv_t[...].T


def join_heads_kernel(
    meta, xr_ref, ctx_own, ctx_oth, wo_own, wo_a, wo_b, gain, mid_ref, n2_a, n2_b, n2_t,
):
    total, width = xr_ref.shape
    half = total // 2
    part = width // 2
    for b in range(0, total, QB):
        span = slice(b, b + QB)
        mid_ref[span, :] = xr_ref[span, :].astype(F32) + dot(
            ctx_own[span, :], wo_own[...]
        )
        for piece, core in ((wo_a, meta[2]), (wo_b, 1 - meta[2])):
            cols = pl.ds(pl.multiple_of(core * part, BLK), part)
            mid_ref[span, cols] += dot(ctx_oth[span, :], piece[...])
        mid = mid_ref[span, :]
        scale = lax.rsqrt(jnp.mean(mid * mid, axis=-1, keepdims=True) + EPS)
        rows = (mid * scale * gain[...]).astype(BF)
        (n2_a if b < half else n2_b)[b % half : b % half + QB, :] = rows
        n2_t[:, span] = rows.T


def turn_kernel(meta, own_ref, oth_a, oth_b, out_a, out_b, out_t, wide):
    half = out_a.shape[0]
    total = 2 * half
    put_halves(wide, own_ref, [oth_a, oth_b], meta[1])
    for b in range(0, total, QB):
        rows = get_rows(wide, meta[0] + b, QB).astype(BF)
        (out_a if b < half else out_b)[b % half : b % half + QB, :] = rows
        out_t[:, b : b + QB] = rows.T


def gelu_parts(pre):
    square = pre * pre
    tanh = jnp.tanh(pre * (GELU_C + GELU_C * GELU_A * square))
    gate = 0.5 + 0.5 * tanh
    slope = gate + pre * (0.5 - 0.5 * tanh * tanh) * (
        GELU_C + 3.0 * GELU_C * GELU_A * square
    )
    return pre * gate, slope


def feed_forward(n2, cotr, up, down, hid, grad, gn_ref, low):
    rows, units = hid.shape
    chunk = up(0).shape[1]
    chunks = range(units // chunk)
    steps = [(b, c) for b in range(0, rows, QB) for c in chunks]

    def front(b, c):
        span, cols = slice(b, b + QB), slice(c * chunk, (c + 1) * chunk)
        value, slope = gelu_parts(dot(n2[span, :], up(c)))
        back = dot_nt(cotr[span, :], down(c))
        hid[span, cols] = value.astype(BF)
        grad[span, cols] = (back * slope).astype(BF)

    def products(b):
        span = slice(b, b + QB)
        parts = [(hid[span, c * chunk : (c + 1) * chunk],
                  grad[span, c * chunk : (c + 1) * chunk], c) for c in chunks]
        gn_ref[span, :] = sum(dot_nt(g, up(c)) for _, g, c in parts)
        low[span, :] = sum(dot(h, down(c)) for h, _, c in parts)

    front(*steps[0])
    for n, (b, c) in enumerate(steps):
        if n + 1 < len(steps):
            front(*steps[n + 1])
        if c == chunks[-1]:
            products(b)


def feed_kernel(n2, w_up, w_down, hid, slope_ref, low):
    rows, units = hid.shape
    chunk = units // 2
    steps = [(b, c) for b in range(0, rows, QB) for c in range(0, units, chunk)]

    def front(b, c):
        span, cols = slice(b, b + QB), slice(c, c + chunk)
        value, slope = gelu_parts(dot(n2[span, :], w_up[:, cols]))
        hid[span, cols] = value.astype(BF)
        slope_ref[span, cols] = slope.astype(BF)

    front(*steps[0])
    for n, (b, c) in enumerate(steps):
        if n + 1 < len(steps):
            front(*steps[n + 1])
        if c + chunk == units:
            span = slice(b, b + QB)
            low[span, :] = dot(hid[span, :], w_down[...])


def feed_back_kernel(cotr, slope_ref, w_up, w_down, grad, gn_ref):
    rows, units = grad.shape
    chunk = units // 2
    steps = [(b, c) for b in range(0, rows, QB) for c in range(0, units, chunk)]

    def front(b, c):
        span, cols = slice(b, b + QB), slice(c, c + chunk)
        back = dot_nt(cotr[span, :], w_down[cols, :])
        grad[span, cols] = (back * slope_ref[span, cols].astype(F32)).astype(BF)

    front(*steps[0])
    for n, (b, c) in enumerate(steps):
        if n + 1 < len(steps):
            front(*steps[n + 1])
        if c + chunk == units:
            span = slice(b, b + QB)
            gn_ref[span, :] = dot_nt(grad[span, :], w_up[...])


def ffn_oth_kernel(meta, n2, cotr, keep, got, gn_ref, low, hid, grad, w_up, w_down):
    for core, (up_ref, down_ref) in enumerate(((keep, got), (got, keep))):

        @pl.when(meta[2] == core)
        def _():
            w_up[...] = up_ref[...]
            w_down[...] = down_ref[...]

    chunk = hid.shape[1] // 2

    def up(c):
        return w_up[:, c * chunk : (c + 1) * chunk]

    def down(c):
        return w_down[:, c * chunk : (c + 1) * chunk]

    feed_forward(n2, cotr, up, down, hid, grad, gn_ref, low)


def output_kernel(meta, low_a, low_b, oth_a, oth_b, mid_ref, out_ref, wide):
    total = mid_ref.shape[0]
    half = total // 2
    for n, (low, oth) in enumerate(((low_a, oth_a), (low_b, oth_b))):
        for b in range(0, half, QB):
            span = slice(b, b + QB)
            rows = slice(n * half + b, n * half + b + QB)
            put_rows(wide, n * half + b, mid_ref[rows, :] + (low[span, :] + oth[span, :]))
    at = total - meta[0] + meta[1] * half
    for b in range(0, half, QB):
        out_ref[b : b + QB, :] = get_rows(wide, at + b, QB).astype(BF)


def ffn_grads_kernel(
    meta, n2_t, cot_t, hid_a, hid_b, grad_a, grad_b, keep_ref, send_ref
):
    half, chunk = hid_a.shape[0], cot_t.shape[0]
    for core in range(2):

        @pl.when(meta[2] == core)
        def _():
            up_ref, down_ref = (keep_ref, send_ref) if core == 0 else (send_ref, keep_ref)
            for c in range(0, hid_a.shape[1], chunk):
                cols = slice(c, c + chunk)
                up_ref[:, cols] = (
                    dot(n2_t[:, :half], grad_a[:, cols])
                    + dot(n2_t[:, half:], grad_b[:, cols])
                ).astype(BF)
                down = dot(cot_t[:, :half], hid_a[:, cols]) + dot(
                    cot_t[:, half:], hid_b[:, cols]
                )
                down_ref[:, cols] = down.T.astype(BF)


def flip_kernel(x_ref, out_ref):
    for b in range(0, x_ref.shape[0], QB):
        out_ref[:, b : b + QB] = x_ref[b : b + QB, :].T


def middle_kernel(
    meta, own_a, own_b, oth_a, oth_b, mid_ref, cotr_a, cotr_b, gain_two,
    gm_ref, gm_own, small_ref,
    wide,
):
    total, width = mid_ref.shape
    half = total // 2
    gain_acc = jnp.zeros((1, width), F32)
    for b in range(0, total, QB):
        span = slice(b, b + QB)
        at = slice(b % half, b % half + QB)
        own = (own_a if b < half else own_b)[at, :]
        mid = mid_ref[span, :]
        e = own + (oth_a if b < half else oth_b)[at, :].astype(F32)
        scale = lax.rsqrt(jnp.mean(mid * mid, axis=-1, keepdims=True) + EPS)
        se = gain_two[...] * e
        mean = jnp.mean(se * mid, axis=-1, keepdims=True)
        grad = (cotr_a if b < half else cotr_b)[at, :].astype(F32) + (
            scale * se - mid * (scale * scale * scale * mean)
        )
        gm_ref[span, :] = grad.astype(BF)
        put_rows(wide, b, grad)
        gain_acc = gain_acc + jnp.sum(own * mid * scale, axis=0, keepdims=True)
    small_ref[...] = jnp.broadcast_to(gain_acc, small_ref.shape)
    back = total - meta[0]
    for b in range(0, half, QB):
        gm_own[b : b + QB, :] = get_rows(wide, back + meta[1] * half + b, QB)


def attn_bwd_kernel(
    band,
    gm, wo_ref, q_ref, k_ref, v_ref, ctx_ref, inv_ref, pl_ref, pt_ref,
    dq_ref, dk_ref, dv_ref, go_ref, ds_ref, sum_ref,
    ds_long, ds_tail, do_ref, kt_ref, dq_t, inner_ref, do_all, dkv_ref,
):
    total, long = gm.shape[0], pl_ref.shape[1]
    index = {pair: n for n, pair in enumerate(band)}
    lane = lax.broadcasted_iota(jnp.int32, (total, 2 * HD), 1)
    do = dot_nt(gm[...], wo_ref[...]).astype(BF).astype(F32) * inv_ref[...]
    do = do.astype(BF)
    k_t = k_ref[...].T
    inner_t = (do.astype(F32) * ctx_ref[...].astype(F32)).T
    inner = []
    extra = kt_ref.shape[1] - HD
    marks = lax.broadcasted_iota(jnp.int32, (extra, total), 0)
    marks = marks == lax.broadcasted_iota(jnp.int32, (extra, total), 1) // BLK
    marks = jnp.where(marks, 1.0, 0.0).astype(BF)
    for hh in range(2):
        do_ref[hh] = jnp.where((lane < HD) == (hh == 0), do, jnp.zeros_like(do))
        kt_ref[hh, 0:HD, :] = k_t[hh * HD : (hh + 1) * HD, :]
        kt_ref[hh, HD:, :] = marks
        inner.append(jnp.sum(inner_t[hh * HD : (hh + 1) * HD, :], axis=0, keepdims=True))
    inner_ref[...] = jnp.concatenate(
        [jnp.broadcast_to(rows, (8, total)) for rows in inner], axis=0
    )

    def head(hh, carry):
        rows_of_head = pl.ds(pl.multiple_of(hh * HD, HD), HD)
        row = inner_ref[pl.ds(pl.multiple_of(hh * 8, 8), 8), :][0:1, :]
        for start in range(0, total, QB):
            lo, hi = (0, long) if start < long else (long, total)
            terms, ds_here = (pl_ref, ds_long) if start < long else (pt_ref, ds_tail)
            cols = slice(start - lo, start - lo + QB)
            for j in range(lo, hi, BLK):
                rows = slice(j - lo, j - lo + BLK)
                dp = dot_nt(v_ref[j : j + BLK, :], do_ref[hh, start : start + QB, :])
                ds = terms[hh, rows, cols].astype(F32) * (dp - row[:, start : start + QB])
                ds = ds.astype(BF)
                ds_here[rows, cols] = ds
                for c in range(0, QB, BLK):
                    pair = (j // BLK, (start + c) // BLK)
                    if pair in index:
                        ds_ref[hh, index[pair]] = ds[:, c : c + BLK]
            sums = dot(kt_ref[hh, :, lo:hi], ds_here[:, cols])
            dq_t[rows_of_head, start : start + QB] = sums[0:HD, :]
            sum_ref[hh, :, start : start + QB] = sums[HD:, :]
        for lo, hi, ds_here, terms in (
            (0, long, ds_long, pl_ref), (long, total, ds_tail, pt_ref)
        ):
            dkv_ref[hh, 0, lo:hi, :] = dot(ds_here[...], q_ref[lo:hi, :])
            dkv_ref[hh, 1, lo:hi, :] = dot(terms[hh], do_all[lo:hi, :])
        return carry

    do_all[...] = do
    lax.fori_loop(0, 2, head, 0)
    dq = dq_t[...].T * HD ** (-0.5)
    dk = jnp.where(lane < HD, dkv_ref[0, 0], dkv_ref[1, 0])
    dv = jnp.where(lane < HD, dkv_ref[0, 1], dkv_ref[1, 1])
    dq_ref[...] = dq.astype(BF)
    dk_ref[...] = dk.astype(BF)
    dv_ref[...] = dv.astype(BF)
    go_ref[...] = dot(ctx_ref[...].T, gm[...]).astype(BF)


def grads_kernel(pairs, meta, nx_t, *refs):
    pieces, go_pieces = refs[: 3 * pairs], refs[3 * pairs : 4 * pairs]
    keep_ref, send_ref, dqkv = refs[4 * pairs :]
    rows, local = keep_ref.shape[0], pairs * 2 * HD
    for n, piece in enumerate(pieces):
        dqkv[:, n * BLK : (n + 1) * BLK] = piece[...]
    for core in range(2):

        @pl.when(meta[2] == core)
        def _():
            for out, part in ((send_ref, 1 - core), (keep_ref, core)):
                grad = dot(nx_t[part * rows : (part + 1) * rows, :], dqkv[...])
                out[:, : 3 * local] = grad.astype(BF)
                for n, piece in enumerate(go_pieces):
                    out[n * BLK : (n + 1) * BLK, 3 * local :] = piece[
                        :, part * rows : (part + 1) * rows
                    ]


def normed_kernel(pairs, meta, xr_ref, dqkv, wq, wk, wv, gn_own, gn_send, small_ref, wide):
    total, width = xr_ref.shape
    half, local = total // 2, pairs * 2 * HD
    gain_acc = jnp.zeros((1, width), F32)
    for b in range(0, total, QB):
        span = slice(b, b + QB)
        back = sum(
            dot_nt(dqkv[span, n * local : (n + 1) * local], w[...])
            for n, w in enumerate((wq, wk, wv))
        )
        x = xr_ref[span, :].astype(F32)
        scale = lax.rsqrt(jnp.mean(x * x, axis=-1, keepdims=True) + EPS)
        gain_acc = gain_acc + jnp.sum(back * x * scale, axis=0, keepdims=True)
        put_rows(wide, b, back)
    small_ref[...] = jnp.broadcast_to(gain_acc, small_ref.shape)
    at = total - meta[0]
    for b in range(0, half, QB):
        gn_own[b : b + QB, :] = get_rows(wide, at + meta[1] * half + b, QB)
        gn_send[b : b + QB, :] = get_rows(
            wide, at + (1 - meta[1]) * half + b, QB
        ).astype(BF)


def table_kernel(diagonal, blocks, bkt_ref, ds_ref, sum_ref, out_ref):
    lane = lax.broadcasted_iota(jnp.int32, (8, BLK), 1)
    levels, tiles = BUCKETS // 2, BLK // 8
    beside = (ds_ref.shape[1] - diagonal) // 2

    def counted(wanted, n, hh, sums):
        cells = ds_ref[hh, n].astype(F32).reshape(tiles, 8, BLK)
        bucket = bkt_ref[n].reshape(tiles, 8, BLK)
        return tuple(
            total
            + jnp.sum(jnp.where(bucket[r0:r1] == b, cells[r0:r1], 0.0), axis=0)
            for total, (b, r0, r1) in zip(sums, wanted)
        )

    reach = [b if b < levels // 2 else LIMITS[b - levels // 2] - 1 for b in range(levels - 1)]
    spans = [sum(8 * r + 1 <= n for r in range(tiles)) for n in reach[1:]] + [tiles]
    parts = (
        (0, diagonal, [(b, 0, tiles) for b in range(BUCKETS) if b != levels]),
        (diagonal, beside, [(levels + 1 + n, 0, s) for n, s in enumerate(spans)]),
        (diagonal + beside, beside, [(1 + n, tiles - s, tiles) for n, s in enumerate(spans)]),
    )
    zero = jnp.zeros((8, BLK), F32)

    def head(hh, carry):
        sums = [zero] * BUCKETS
        for first, count, wanted in parts:
            found = lax.fori_loop(
                first,
                first + count,
                lambda n, part, wanted=wanted: counted(wanted, n, hh, part),
                (zero,) * len(wanted),
            )
            for (b, _, _), part in zip(wanted, found):
                sums[b] = sums[b] + part
        for i in range(blocks):
            cols = sum_ref[hh, 0:8, i * BLK : (i + 1) * BLK]
            key_block = lax.broadcasted_iota(jnp.int32, (8, BLK), 0)
            far = (key_block < blocks) & (jnp.abs(key_block - i) > 1)
            for b, side in ((levels - 1, key_block < i), (BUCKETS - 1, key_block > i)):
                sums[b] = sums[b] + jnp.where(far & side, cols, 0.0)
        row = zero
        for b in range(BUCKETS):
            row = jnp.where(lane == b, jnp.sum(sums[b]), row)
        out_ref[hh] = row
        return carry

    lax.fori_loop(0, 2, head, 0)


def final_kernel(
    x_ref, gain, gn_own, gn_oth, gm_ref, grad_ref
):
    for b in range(0, x_ref.shape[0], QB):
        span = slice(b, b + QB)
        x = x_ref[span, :].astype(F32)
        e = gn_own[span, :] + gn_oth[span, :].astype(F32)
        scale = lax.rsqrt(jnp.mean(x * x, axis=-1, keepdims=True) + EPS)
        se = gain[...] * e
        mean = jnp.mean(se * x, axis=-1, keepdims=True)
        grad_ref[span, :] = (
            gm_ref[span, :] + (scale * se - x * (scale * scale * scale * mean))
        ).astype(BF)


def add_kernel(at, meta, keep, got, *outs):
    rows = outs[0].shape[0]
    if len(outs) == 1:
        outs[0][...] = (keep[...].astype(F32) + got[...].astype(F32)).astype(BF)
        return
    for out, part in ((outs[0], meta[at]), (outs[1], 1 - meta[at])):
        span = pl.ds(pl.multiple_of(part * rows, 16), rows)
        out[...] = (keep[span, :].astype(F32) + got[span, :].astype(F32)).astype(BF)


def join_kernel(at, meta, mine, got, out):
    rows = mine.shape[0]
    out[pl.ds(pl.multiple_of(meta[at] * rows, 16), rows), :] = mine[...]
    out[pl.ds(pl.multiple_of((1 - meta[at]) * rows, 16), rows), :] = got[...]


def little_kernel(a_ref, b_ref, out_ref):
    out_ref[...] = a_ref[...] + b_ref[...]


def split_ffn_kernel(meta, mine, got, up_ref, down_ref):
    width = down_ref.shape[1]
    for core in range(2):

        @pl.when(meta[2] == core)
        def _():
            up, down = (mine, got) if core == 0 else (got, mine)
            up_ref[...] = up[...].astype(F32)
            for n in range(down.shape[1] // width):
                rows = slice(n * down.shape[0], (n + 1) * down.shape[0])
                down_ref[rows, :] = down[:, n * width : (n + 1) * width].astype(F32)


def split_attn_kernel(meta, mine, got, q_ref, k_ref, v_ref, o_ref):
    rows, local = mine.shape[0], q_ref.shape[1]
    for core in range(2):

        @pl.when(meta[2] == core)
        def _():
            for n, part in enumerate((mine, got) if core == 0 else (got, mine)):
                span = slice(n * rows, (n + 1) * rows)
                for m, out in enumerate((q_ref, k_ref, v_ref)):
                    out[span, :] = part[:, m * local : (m + 1) * local].astype(F32)
                o_ref[:, span] = part[:, 3 * local :].astype(F32)


def swap(value, size, flip, axis="dp"):
    return lax.ppermute(value, axis, [(n, flip(n)) for n in range(size)])


class Exchange:
    def __init__(self, name, meta, size, orders):
        self.name, self.meta, self.size, self.orders = name, meta, size, orders
        self.phase, self.joins, self.waiting = -1, [], -2

    def gather(self, piece, cuts):
        self.keep, self.joins = piece, list(range(cuts))
        self.back()
        return self

    def sum(self, keep, send):
        self.keep = keep
        self.got = swap(send, self.size, lambda n: n ^ 1)
        return self

    def flip(self, phase):
        if phase < 0:
            return lambda n: n ^ 1
        orders = self.orders
        return lambda n: n ^ (1 << orders[n & 1][phase])

    def pair(self, value):
        return (value, full(value.shape))

    def reduce(self, after=()):
        self.phase += 1
        shape = self.keep.shape
        last = self.phase == len(self.orders[0])
        cut = not last and shape[0] % 32 == 0
        rows = shape[0] // 2 if cut else shape[0]
        out = (jax.ShapeDtypeStruct((rows, shape[1]), BF), full((rows, shape[1])))
        parts = call(
            functools.partial(add_kernel, 3 + self.phase),
            [(self.meta, smem()), self.pair(self.keep), self.pair(self.got)],
            [out, out] if cut else [out],
            name=f"{self.name}_add{self.phase}",
            after=after,
        )
        self.keep = parts[0]
        if last:
            self.back()
            return self.keep
        if cut:
            self.joins.append(self.phase)
        self.got = swap(parts[-1], self.size, self.flip(self.phase))
        return self.keep

    def back(self, parts=1):
        phase = self.joins.pop() if self.joins else -1
        self.waiting = phase
        if phase < 0 and parts > 1:
            self.got = [
                swap(v, self.size, self.flip(phase))
                for v in jnp.split(self.keep, parts, axis=1)
            ]
            return
        self.got = swap(self.keep, self.size, self.flip(phase))

    def join(self, after=(), parts=1):
        rows, cols = self.keep.shape
        self.keep = call(
            functools.partial(join_kernel, 3 + self.waiting),
            [(self.meta, smem()), self.pair(self.keep), self.pair(self.got)],
            [(jax.ShapeDtypeStruct((2 * rows, cols), BF), full((2 * rows, cols)))],
            name=f"{self.name}_join{self.waiting}",
            after=after,
        )[0]
        self.back(parts)
        return self.keep


def body(
    inputs, norm_one, w_query, w_key, w_value, w_out, bias_table, norm_two, w_up, w_down,
    doc_lengths, layout_steps, cotangent, *, size,
):
    row_len = layout_steps.shape[0]
    half, width = inputs.shape
    long = 3 * row_len // 4
    local = w_query.shape[1]
    pairs = local // (2 * HD)
    hidden_units = w_up.shape[1]
    mp = lax.axis_index("mp")
    dp = lax.axis_index("dp")
    core = dp & 1
    band = band_blocks(long // BLK, row_len // BLK)
    count = len(band)

    def other(value):
        return swap(value, 2, lambda n: 1 - n, "mp")

    def core_swap(value):
        return swap(value, size, lambda n: n ^ 1)

    doc_ends = jnp.cumsum(doc_lengths[0])
    turn = jnp.sum(
        jnp.where(doc_lengths[0] == long, doc_ends - doc_lengths[0], 0)
    ).astype(jnp.int32)
    places = jnp.arange(row_len, dtype=jnp.int32)
    segment = jnp.sum((places[:, None] >= doc_ends[None, :]).astype(jnp.int32), axis=1)
    position = jnp.cumsum(layout_steps)
    both = jnp.stack([position, segment])
    both = lax.dynamic_slice_in_dim(
        jnp.concatenate([both, both], axis=1), turn, row_len, 1
    ).astype(jnp.int32)

    table = jnp.pad(bias_table.T, ((0, 8 - bias_table.shape[1]), (0, 0)))
    table = jnp.concatenate(
        [table, jnp.full((8, BLK - BUCKETS), MASKED, F32)], axis=1
    )
    gain_one, gain_two = norm_one.reshape(1, width), norm_two.reshape(1, width)

    depth = size.bit_length() - 1
    rest = list(range(1, depth))
    orders = (rest, rest[1:] + rest[:1])
    bits = [(dp >> b) & 1 for b in range(depth)]
    phase_bits = [
        jnp.where(core == 0, bits[orders[0][t]], bits[orders[1][t]])
        for t in range(depth - 1)
    ]
    meta = jnp.stack([turn, mp, core] + phase_bits).astype(jnp.int32)

    shape = jax.ShapeDtypeStruct
    heads = 2 * pairs
    tail = row_len - long
    part = width // 2
    pair_block = pl.BlockSpec((row_len, 2 * HD), lambda p: (0, p))
    weight_block = pl.BlockSpec((width, 2 * HD), lambda p: (0, p))

    def whole(value):
        return (value, full(value.shape))

    def out(dims, kind=BF, spec=None):
        return (shape(dims, kind), spec or full(dims))

    def cuts_of(rows):
        cuts = 0
        while cuts < depth - 1 and rows % 32 == 0:
            rows, cuts = rows // 2, cuts + 1
        return cuts, rows

    def piece_of(rows):
        cuts, least = cuts_of(rows)
        return sum(phase_bits[t] * (rows // least >> (t + 1)) for t in range(cuts))

    ffn_cuts, ffn_rows = cuts_of(width)
    at = jnp.stack([piece_of(width), core]).astype(jnp.int32)
    anywhere = pl.BlockSpec(memory_space=pl.ANY)
    x_oth = other(inputs)
    early = 3 * half // 8
    ffn_piece, wo_send, cot_a = call(
        pieces_kernel,
        [
            (at, smem()), (w_out, anywhere), (w_up, anywhere), (w_down, anywhere),
            (cotangent, anywhere),
        ],
        [out((ffn_rows, hidden_units)), out((local, part)), out((early, width))],
        name="pieces",
        scratch=[pltpu.SemaphoreType.DMA((4,))],
        limit=VMEM_LIMIT,
        after=[both, meta, table, gain_one, gain_two],
    )
    ffn_piece = other(ffn_piece)
    wo_a = other(wo_send)
    cot_a = other(cot_a)

    work = [
        pltpu.VMEM((2, long, QB), F32),
        pltpu.VMEM((2, HD + 16, row_len), BF),
        pltpu.VMEM((2, row_len, 2 * HD), BF),
        pltpu.VMEM((row_len, 2 * HD), BF),
        pltpu.VMEM((2 * HD, row_len), F32),
    ]
    wide = pltpu.VMEM((width // BLK, 2 * row_len, BLK), F32)
    long_spec = pl.BlockSpec((2, long, long), lambda p: (p, 0, 0))
    tail_spec = pl.BlockSpec((2, tail, tail), lambda p: (p, 0, 0))
    xr, nx, qs, keys, values, ctx_own, inv, p_long, p_tail, bkt = call(
        functools.partial(attn_own_kernel, long, band),
        [
            (meta, smem()), whole(inputs), whole(x_oth), whole(gain_one), whole(both),
            (w_query, weight_block), (w_key, weight_block), (w_value, weight_block),
            whole(table),
        ],
        [
            out((row_len, width)), out((row_len, width)),
            out((row_len, local), BF, pair_block), out((row_len, local), BF, pair_block),
            out((row_len, local), BF, pair_block), out((row_len, local), BF, pair_block),
            out((row_len, local), F32, pair_block), out((heads, long, long), BF, long_spec),
            out((heads, tail, tail), BF, tail_spec), out((count, BLK, BLK), jnp.int32),
        ],
        name="attend_own",
        grid=(pairs,),
        scratch=[wide] + work + [pltpu.VMEM((2 * HD, row_len), F32)],
    )

    ctx_send, ffn_piece, wo_a, cot_a = call(
        copy_kernel,
        [whole(v) for v in (ctx_own, ffn_piece, wo_a, cot_a)],
        [out(v.shape) for v in (ctx_own, ffn_piece, wo_a, cot_a)],
        name="take_pieces",
    )
    ctx_oth = other(ctx_send)
    (cot_send,) = call(
        copy_kernel, [whole(cotangent[early:])], [out((half - early, width))],
        name="take_cotangent", after=[ctx_send],
    )
    cot_b = other(cot_send)
    ffn_w = Exchange("ffn_w", meta, size, orders).gather(ffn_piece, ffn_cuts)
    wo_b = core_swap(wo_a)
    mark = wo_b
    if ffn_w.waiting >= 0:
        mark = ffn_w.join([wo_b])

    mid, n2_a, n2_b, n2_t = call(
        join_heads_kernel,
        [
            (meta, smem()), whole(xr), whole(ctx_own), whole(ctx_oth), whole(w_out),
            whole(wo_a), whole(wo_b), whole(gain_two),
        ],
        [
            out((row_len, width), F32), out((half, width)), out((half, width)),
            out((width, row_len)),
        ],
        name="join_heads",
        after=[mark],
    )
    n2 = (n2_a, n2_b)
    mark = n2_b
    hid, slopes, low = [], [], []
    for h in range(2):
        hid_h, slope_h, low_h = call(
            feed_kernel,
            [whole(n2[h]), whole(w_up), whole(w_down)],
            [out((half, hidden_units)), out((half, hidden_units)), out((half, width), F32)],
            name=f"feed{h}",
            after=[mark],
        )
        mark = low_h
        hid.append(hid_h)
        slopes.append(slope_h)
        low.append(low_h)
    *cotr, cot_t = call(
        turn_kernel,
        [(meta, smem()), whole(cotangent), whole(cot_a), whole(cot_b)],
        [out((half, width)), out((half, width)), out((width, row_len))],
        name="turn_cotangent",
        scratch=[wide],
        after=[mark],
    )
    mark = cot_t
    if ffn_w.waiting >= 0 and ffn_w.joins:
        mark = ffn_w.join([mark])
    grad_pre, gn2_own, gn2_oth, low_oth = [], [], [], []
    for h in range(2):
        grad_h, own_h = call(
            feed_back_kernel,
            [whole(cotr[h]), whole(slopes[h]), whole(w_up), whole(w_down)],
            [out((half, hidden_units)), out((half, width), F32)],
            name=f"feed_back{h}",
            after=[mark],
        )
        mark = own_h
        grad_pre.append(grad_h)
        gn2_own.append(own_h)
    ffn_keep, ffn_send = call(
        ffn_grads_kernel,
        [(meta, smem()), whole(n2_t), whole(cot_t)] + [whole(v) for v in hid + grad_pre],
        [out((width, hidden_units)), out((width, hidden_units))],
        name="ffn_grads",
        after=[mark],
    )
    ffn = Exchange("ffn", meta, size, orders).sum(ffn_keep, ffn_send)
    mark = ffn_keep
    while ffn_w.waiting >= 0:
        mark = ffn_w.join([mark])
    mark = ffn.reduce([mark])
    for h in range(2):
        oth_h, low_h = call(
            ffn_oth_kernel,
            [
                (meta, smem()), whole(n2[h]), whole(cotr[h]), whole(ffn_w.keep),
                whole(ffn_w.got),
            ],
            [out((half, width), F32), out((half, width), F32)],
            name=f"feed_oth{h}",
            scratch=[
                pltpu.VMEM((half, hidden_units), BF),
                pltpu.VMEM((half, hidden_units), BF),
                pltpu.VMEM((width, hidden_units), BF),
                pltpu.VMEM((width, hidden_units), BF),
            ],
            after=[mark],
        )
        mark = low_h
        gn2_oth.append(oth_h)
        low_oth.append(low_h)
    mark = mark_one = ffn.reduce([mark])
    (nx_t,) = call(
        flip_kernel, [whole(nx)], [out((width, row_len))], name="flip", after=[mark]
    )

    gm, gm_own, small_two = call(
        middle_kernel,
        [(meta, smem())]
        + [whole(v) for v in gn2_own + gn2_oth]
        + [whole(mid)]
        + [whole(v) for v in cotr]
        + [whole(gain_two)],
        [out((row_len, width)), out((half, width), F32), out((8, width), F32)],
        name="grad_middle",
        scratch=[wide],
        after=[nx_t],
    )
    tables = []

    def table_sums(p, after):
        (sums,) = call(
            functools.partial(table_kernel, row_len // BLK, long // BLK),
            [whole(bkt), whole(ds_pieces[p]), whole(sum_pieces[p])],
            [out((2, 8, BLK), F32)],
            name=f"table_sums{p}",
            after=after,
        )
        tables.append(sums)
        return sums

    pieces, go_pieces, ds_pieces, sum_pieces = [], [], [], []
    for p in range(pairs):
        pair = pl.BlockSpec((row_len, 2 * HD), lambda *_, p=p: (0, p))
        dq, dk, dv, go, ds, sums = call(
            functools.partial(attn_bwd_kernel, band),
            [
                whole(gm), (w_out, pl.BlockSpec((2 * HD, width), lambda *_, p=p: (p, 0))),
                (qs, pair), (keys, pair), (values, pair), (ctx_own, pair), (inv, pair),
                (p_long, pl.BlockSpec((2, long, long), lambda *_, p=p: (p, 0, 0))),
                (p_tail, pl.BlockSpec((2, tail, tail), lambda *_, p=p: (p, 0, 0))),
            ],
            [
                out((row_len, 2 * HD)), out((row_len, 2 * HD)), out((row_len, 2 * HD)),
                out((2 * HD, width)), out((2, count, BLK, BLK)), out((2, 16, row_len), F32),
            ],
            name=f"attend_back{p}",
            scratch=[
                pltpu.VMEM((long, long), BF),
                pltpu.VMEM((tail, tail), BF),
                pltpu.VMEM((2, row_len, 2 * HD), BF),
                pltpu.VMEM((2, HD + 16, row_len), BF),
                pltpu.VMEM((2 * HD, row_len), F32),
                pltpu.VMEM((16, row_len), F32),
                pltpu.VMEM((row_len, 2 * HD), BF),
                pltpu.VMEM((2, 2, row_len, 2 * HD), F32),
            ],
            after=[mark],
        )
        pieces.append((dq, dk, dv))
        go_pieces.append(go)
        ds_pieces.append(ds)
        sum_pieces.append(sums)
        mark = dq
        if p == 1:
            for _ in range(depth - 3):
                mark = ffn.reduce([mark])
    mark = table_sums(0, [mark])
    mark = ffn.reduce([mark])
    operands = [whole(pieces[p][n]) for n in range(3) for p in range(pairs)]
    attn_keep, attn_send, dqkv = call(
        functools.partial(grads_kernel, pairs),
        [(meta, smem()), whole(nx_t)] + operands + [whole(go) for go in go_pieces],
        [
            out((part, 3 * local + part)), out((part, 3 * local + part)),
            out((row_len, 3 * local)),
        ],
        name="attend_grads",
        after=[mark],
    )
    attn = Exchange("attn", meta, size, orders).sum(attn_keep, attn_send)
    gn_own, gn_send, small_one = call(
        functools.partial(normed_kernel, pairs),
        [
            (meta, smem()), whole(xr), whole(dqkv), whole(w_query), whole(w_key),
            whole(w_value),
        ],
        [out((half, width), F32), out((half, width)), out((8, width), F32)],
        name="grad_normed",
        scratch=[wide],
    )
    gn_oth = other(gn_send)
    gains = jnp.concatenate([small_one[0:1], small_two[0:1]], axis=0)
    gains = gains.reshape(2 * width // BLK, BLK)
    gains_oth = other(gains)

    def join_ffn(after):
        return ffn.join([after]) if ffn.waiting >= 0 else after

    mark = attn.reduce([small_one])
    mark = table_sums(1, [mark])
    mark = join_ffn(mark)
    mark = attn.reduce([mark])
    for p in range(2, pairs):
        mark = table_sums(p, [mark])
    while attn.phase < depth - 2:
        mark = attn.reduce([mark, gains_oth])
    little = jnp.concatenate([gains + gains_oth] + [t[:, 0, :] for t in tables], axis=0)
    (output,) = call(
        output_kernel,
        [(meta, smem())] + [whole(v) for v in low + low_oth] + [whole(mid)],
        [out((half, width))],
        name="output",
        scratch=[wide],
        limit=VMEM_LIMIT,
        after=[mark],
    )
    mark = attn.reduce([output, gn_oth])
    got, phase = swap(little, size, attn.flip(0)), 0

    def little_step(after):
        nonlocal little, got, phase
        little = call(
            little_kernel,
            [whole(little), whole(got)],
            [out(little.shape, F32)],
            name=f"little{phase}",
            after=[after],
        )[0]
        phase += 1
        if phase < depth:
            got = swap(little, size, attn.flip(phase if phase < depth - 1 else -1))
        return little

    mark = join_ffn(mark)
    mark = attn.join([mark]) if attn.waiting >= 0 else mark
    mark = little_step(mark)
    while attn.waiting > 0:
        mark = attn.join([mark])
        if phase < depth - 1:
            mark = little_step(mark)
    while phase < depth - 1:
        mark = little_step(mark)
    while ffn.waiting >= 0:
        mark = ffn.join([mark])
    (input_grad,) = call(
        final_kernel,
        [
            whole(inputs), whole(gain_one), whole(gn_own), whole(gn_oth), whole(gm_own),
        ],
        [out((half, width))],
        name="input_grad",
        after=[mark],
    )
    grad_up, grad_down = call(
        split_ffn_kernel,
        [(meta, smem()), whole(ffn.keep), whole(ffn.got)],
        [out((width, hidden_units), F32), out((hidden_units, width), F32)],
        name="ffn_split",
        after=[input_grad],
    )
    mark = grad_up
    if attn.waiting >= 0:
        mark = attn.join([mark])
    little_step(mark)
    grad_query, grad_key, grad_value, grad_out = call(
        split_attn_kernel,
        [(meta, smem()), whole(attn.keep), whole(attn.got)],
        [
            out((width, local), F32), out((width, local), F32), out((width, local), F32),
            out((local, width), F32),
        ],
        name="attn_split",
    )
    gains = little[: 2 * width // BLK].reshape(2, width)
    grad_table = little[2 * width // BLK :, :BUCKETS].T
    return (
        output, input_grad, gains[0], gains[1], grad_query, grad_key, grad_value,
        grad_out, grad_table, grad_up, grad_down,
    )


def solution(mesh):
    placed = (
        P(("dp", "mp"), None),
        P(),
        P(None, "mp"),
        P(None, "mp"),
        P(None, "mp"),
        P("mp", None),
        P(None, "mp"),
        P(),
        P(None, "mp"),
        P("mp", None),
        P("dp", None),
        P("dp"),
        P(("dp", "mp"), None),
    )
    return jax.shard_map(
        functools.partial(body, size=mesh.shape["dp"]),
        mesh=mesh,
        in_specs=placed,
        out_specs=(
            P(("dp", "mp"), None),
            P(("dp", "mp"), None),
            P(),
            P(),
            P(None, "mp"),
            P(None, "mp"),
            P(None, "mp"),
            P("mp", None),
            P(None, "mp"),
            P(None, "mp"),
            P("mp", None),
        ),
        check_vma=False,
    )
```

```python
import functools

import jax
import jax.numpy as jnp
from jax import lax
from jax.experimental import pallas as pl
from jax.experimental.pallas import tpu as pltpu
from jax.sharding import PartitionSpec as P

HD = 64
BUCKETS = 32
MAX_DIST = 128
EPS = 1e-06
MASKED = -1000000000.0
BLK = 128
QB = 256
CUT = 64
GELU_C = 0.7978845608028654
GELU_A = 0.044715
BF = jnp.bfloat16
F32 = jnp.float32
VMEM_LIMIT = 56 * 1024 * 1024
SPARE = 4 * 1024 * 1024


def bucket_limits(buckets, reach):
    halfway = buckets // 2
    exact_span = halfway // 2
    levels = halfway - exact_span
    limits = []
    for degree in range(1, levels):
        target = exact_span ** (levels - degree) * reach**degree
        candidate = exact_span
        while candidate**levels < target:
            candidate = candidate + 1
        limits.append(candidate)
    return limits


LIMITS = bucket_limits(BUCKETS, MAX_DIST)


def dot(a, b):
    return jnp.dot(a, b, preferred_element_type=F32)


def dot_nt(a, b):
    return lax.dot_general(a, b, (((1,), (1,)), ((), ())), preferred_element_type=F32)


def band_blocks(long_blocks, blocks):
    steps = [n for n in range(blocks - 1) if n + 1 != long_blocks]
    return (
        [(n, n) for n in range(blocks)]
        + [(n + 1, n) for n in steps]
        + [(n, n + 1) for n in steps]
    )


def nbytes(shape, kind):
    if isinstance(kind, jax.ShapeDtypeStruct):
        kind = kind.dtype
    rows = -(-shape[-2] // 16) * 16 if len(shape) > 1 else 8
    lanes = -(-shape[-1] // BLK) * BLK
    lead = 1
    for n in shape[:-2]:
        lead = lead * n
    return lead * rows * lanes * jnp.dtype(kind).itemsize


def call(kernel, operands, outs, *, name, grid=(), scratch=(), after=(), limit=None):
    count = len(operands)

    def run(*refs):
        kernel(*refs[:count], *refs[count + len(after) :])

    arrays = list(operands) + list(outs)
    if not grid and any(
        s.block_shape is not None and tuple(s.block_shape) != v.shape for v, s in arrays
    ):
        grid = (1,)
    need = sum(nbytes(s.shape, s.dtype) for s in scratch if len(s.shape) > 1)
    for value, spec in arrays:
        if spec.block_shape is not None:
            need += (2 if grid else 1) * nbytes(spec.block_shape, value.dtype)
    limit = limit or min(VMEM_LIMIT, need + (need >> 3) + SPARE)
    return pl.pallas_call(
        run,
        grid=grid,
        in_specs=[spec for _, spec in operands]
        + [pl.BlockSpec(memory_space=pl.ANY)] * len(after),
        out_specs=[spec for _, spec in outs],
        out_shape=[kind for kind, _ in outs],
        scratch_shapes=list(scratch),
        compiler_params=pltpu.CompilerParams(
            vmem_limit_bytes=limit, dimension_semantics=("arbitrary",) * len(grid)
        ),
        cost_estimate=pl.CostEstimate(
            flops=1, bytes_accessed=1, transcendentals=0
        ),
        name=name,
    )(*[array for array, _ in operands], *after)


def full(shape):
    return pl.BlockSpec(shape, lambda *_: (0,) * len(shape))


def smem():
    return pl.BlockSpec(memory_space=pltpu.SMEM)


def put_rows(wide, row, value):
    total = wide.shape[1] // 2
    count = value.shape[0]
    for n in range(wide.shape[0]):
        cols = value[:, n * BLK : (n + 1) * BLK]
        wide[n, pl.ds(row, count), :] = cols
        wide[n, pl.ds(row + total, count), :] = cols


def get_rows(wide, row, count):
    return jnp.concatenate(
        [wide[n, pl.ds(row, count), :] for n in range(wide.shape[0])], axis=1
    )


def put_halves(wide, own_ref, oth_refs, mp):
    half = own_ref.shape[0]
    for side, refs in ((mp, [own_ref]), (1 - mp, oth_refs)):
        at = 0
        for ref in refs:
            for b in range(0, ref.shape[0], CUT):
                rows = ref[b : b + CUT, :].astype(F32)
                put_rows(wide, pl.multiple_of(side * half + at + b, CUT), rows)
            at += ref.shape[0]


def write_buckets(bkt_ref, posc, posr, segc, segr, band, long_blocks):
    for n, (j, i) in enumerate(band):
        rows, cols = slice(j * BLK, (j + 1) * BLK), slice(i * BLK, (i + 1) * BLK)
        offset = posc[rows, :] - posr[:, cols]
        distance = jnp.abs(offset)
        bucket = jnp.where(offset > 0, BUCKETS // 2, 0) + jnp.minimum(
            distance, BUCKETS // 4
        )
        for limit in LIMITS:
            bucket = bucket + jnp.where(distance >= limit, 1, 0)
        if j >= long_blocks:
            bucket = jnp.where(segc[rows, :] == segr[:, cols], bucket, BUCKETS)
        bkt_ref[n] = bucket


def attend_pair(p, qs, k, v_t, tab_ref, bkt_ref, p_long, p_tail, work, band):
    scores, values, queries, k_ref, ctx_t, inv_t = work
    long, total = p_long.shape[1], ctx_t.shape[1]
    index = {pair: n for n, pair in enumerate(band)}
    lane = lax.broadcasted_iota(jnp.int32, (total, 2 * HD), 1)
    k_ref[...] = k
    tables = []
    for hh in range(2):
        values[hh, 0:HD, :] = v_t[hh * HD : (hh + 1) * HD, :]
        values[hh, HD:, :] = jnp.ones((values.shape[1] - HD, total), BF)
        queries[hh] = jnp.where((lane < HD) == (hh == 0), qs, jnp.zeros_like(qs))
        row = tab_ref[pl.ds(2 * p + hh, 1), :]
        tables.append(
            (
                jnp.broadcast_to(row, (BLK, BLK)),
                row[:, BUCKETS // 2 - 1 : BUCKETS // 2],
                row[:, BUCKETS - 1 : BUCKETS],
            )
        )
    units = [(hh, start) for hh in range(2) for start in range(0, total, QB)]
    tops = {}

    def span(u):
        return (0, long) if units[u][1] < long else (long, total)

    def score(u, j):
        hh, start = units[u]
        lo = span(u)[0]
        table, behind, ahead = tables[hh]
        cells = dot_nt(k_ref[j : j + BLK, :], queries[hh, start : start + QB, :])
        tops_here = []
        for c in range(0, QB, BLK):
            pair = (j // BLK, (start + c) // BLK)
            if pair in index:
                bias = jnp.take_along_axis(
                    table, bkt_ref[index[pair]], axis=1, mode="promise_in_bounds"
                )
            else:
                bias = ahead if pair[0] > pair[1] else behind
            cell = cells[:, c : c + BLK] + bias
            scores[u % 2, j - lo : j - lo + BLK, c : c + BLK] = cell
            tops_here.append(jnp.max(cell.reshape(BLK // 8, 8, BLK), axis=0))
        top = jnp.concatenate(tops_here, axis=1)
        tops[u] = jnp.maximum(tops[u], top) if u in tops else top

    def term(u, j):
        hh, start = units[u]
        lo = span(u)[0]
        out = p_long if start < long else p_tail
        if j == lo:
            tops[u] = jnp.max(tops[u], axis=0, keepdims=True)
        terms = jnp.exp(scores[u % 2, j - lo : j - lo + BLK, :] - tops[u])
        out[hh, j - lo : j - lo + BLK, start - lo : start - lo + QB] = terms.astype(BF)

    def context(u):
        hh, start = units[u]
        lo, hi = span(u)
        out = p_long if start < long else p_tail
        sums = dot(values[hh, :, lo:hi], out[hh, :, start - lo : start - lo + QB])
        inverse = 1.0 / sums[HD : HD + 1, :]
        rows, cols = slice(hh * HD, (hh + 1) * HD), slice(start, start + QB)
        ctx_t[rows, cols] = sums[0:HD, :] * inverse
        if inv_t is not None:
            inv_t[rows, cols] = jnp.broadcast_to(inverse, (HD, QB))

    for j in range(*span(0), BLK):
        score(0, j)
    for u in range(len(units)):
        ahead_of = list(range(*span(u + 1), BLK)) if u + 1 < len(units) else []
        here = list(range(*span(u), BLK))
        for n in range(max(len(ahead_of), len(here))):
            if n < len(ahead_of):
                score(u + 1, ahead_of[n])
            if n < len(here):
                term(u, here[n])
        context(u)


def pieces_kernel(at, wo, up, down, cot, ffn_ref, out_ref, cot_ref, sems):
    rows, width = ffn_ref.shape[0], down.shape[1]
    part = out_ref.shape[1]
    start = pl.multiple_of(at[0] * rows, 16)
    first = pltpu.make_async_copy(
        wo.at[:, pl.ds(pl.multiple_of(at[1] * part, BLK), part)], out_ref, sems.at[0]
    )
    first.start()
    rows_of_cot = pltpu.make_async_copy(
        cot.at[0 : cot_ref.shape[0], :], cot_ref, sems.at[3]
    )
    rows_of_cot.start()

    @pl.when(at[1] == 0)
    def _():
        copy = pltpu.make_async_copy(up.at[pl.ds(start, rows), :], ffn_ref, sems.at[1])
        copy.start()
        copy.wait()

    @pl.when(at[1] == 1)
    def _():
        copies = [
            pltpu.make_async_copy(
                down.at[pl.ds(n * width + start, rows), :],
                ffn_ref.at[:, n * width : (n + 1) * width],
                sems.at[1 + n],
            )
            for n in range(2)
        ]
        for copy in copies:
            copy.start()
        for copy in copies:
            copy.wait()

    first.wait()
    rows_of_cot.wait()


def copy_kernel(*refs):
    for x_ref, out_ref in zip(refs[: len(refs) // 2], refs[len(refs) // 2 :]):
        out_ref[...] = x_ref[...]


def attn_own_kernel(
    long, band,
    meta, x_own, x_oth, gain, place_ref, wq, wk, wv, tab,
    xr_ref, nx_ref, q_ref, k_ref, v_ref, ctx_ref, inv_ref, pl_ref, pt_ref, bkt_ref,
    wide, scores, vals, queries, keys, ctx_t, inv_t,
):
    p = pl.program_id(0)
    total = xr_ref.shape[0]

    @pl.when(p == 0)
    def _():
        put_halves(wide, x_own, [x_oth], meta[1])
        for b in range(0, total, QB):
            rows = get_rows(wide, meta[0] + b, QB)
            xr_ref[b : b + QB, :] = rows.astype(BF)
            scale = lax.rsqrt(jnp.mean(rows * rows, axis=-1, keepdims=True) + EPS)
            nx_ref[b : b + QB, :] = (rows * scale * gain[...]).astype(BF)
        places = place_ref[...].astype(F32)
        down = [
            jnp.broadcast_to(places[n : n + 1, :], (BLK, total)).T.astype(jnp.int32)
            for n in range(2)
        ]
        write_buckets(
            bkt_ref, down[0], place_ref[0:1, :], down[1], place_ref[1:2, :], band,
            long // BLK,
        )

    nx = nx_ref[...]
    qs = (dot(nx, wq[...]).astype(BF).astype(F32) * HD ** (-0.5)).astype(BF)
    k = dot(nx, wk[...]).astype(BF)
    v = dot(nx, wv[...]).astype(BF)
    q_ref[...] = qs
    k_ref[...] = k
    v_ref[...] = v
    work = (scores, vals, queries, keys, ctx_t, inv_t)
    attend_pair(p, qs, k, v.T, tab, bkt_ref, pl_ref, pt_ref, work, band)
    ctx_ref[...] = ctx_t[...].T.astype(BF)
    inv_ref[...] = inv_t[...].T


def join_heads_kernel(
    meta, xr_ref, ctx_own, ctx_oth, wo_own, wo_a, wo_b, gain, mid_ref, n2_a, n2_b, n2_t,
):
    total, width = xr_ref.shape
    half = total // 2
    part = width // 2
    for b in range(0, total, QB):
        span = slice(b, b + QB)
        mid_ref[span, :] = xr_ref[span, :].astype(F32) + dot(
            ctx_own[span, :], wo_own[...]
        )
        for piece, core in ((wo_a, meta[2]), (wo_b, 1 - meta[2])):
            cols = pl.ds(pl.multiple_of(core * part, BLK), part)
            mid_ref[span, cols] += dot(ctx_oth[span, :], piece[...])
        mid = mid_ref[span, :]
        scale = lax.rsqrt(jnp.mean(mid * mid, axis=-1, keepdims=True) + EPS)
        rows = (mid * scale * gain[...]).astype(BF)
        (n2_a if b < half else n2_b)[b % half : b % half + QB, :] = rows
        n2_t[:, span] = rows.T


def turn_kernel(meta, own_ref, oth_a, oth_b, out_a, out_b, out_t, wide):
    half = out_a.shape[0]
    total = 2 * half
    put_halves(wide, own_ref, [oth_a, oth_b], meta[1])
    for b in range(0, total, QB):
        rows = get_rows(wide, meta[0] + b, QB).astype(BF)
        (out_a if b < half else out_b)[b % half : b % half + QB, :] = rows
        out_t[:, b : b + QB] = rows.T


def gelu_parts(pre):
    square = pre * pre
    tanh = jnp.tanh(pre * (GELU_C + GELU_C * GELU_A * square))
    gate = 0.5 + 0.5 * tanh
    slope = gate + pre * (0.5 - 0.5 * tanh * tanh) * (
        GELU_C + 3.0 * GELU_C * GELU_A * square
    )
    return pre * gate, slope


def feed_forward(n2, cotr, up, down, hid, grad, gn_ref, low):
    rows, units = hid.shape
    chunk = up(0).shape[1]
    chunks = range(units // chunk)
    steps = [(b, c) for b in range(0, rows, QB) for c in chunks]

    def front(b, c):
        span, cols = slice(b, b + QB), slice(c * chunk, (c + 1) * chunk)
        value, slope = gelu_parts(dot(n2[span, :], up(c)))
        back = dot_nt(cotr[span, :], down(c))
        hid[span, cols] = value.astype(BF)
        grad[span, cols] = (back * slope).astype(BF)

    def products(b):
        span = slice(b, b + QB)
        parts = [(hid[span, c * chunk : (c + 1) * chunk],
                  grad[span, c * chunk : (c + 1) * chunk], c) for c in chunks]
        gn_ref[span, :] = sum(dot_nt(g, up(c)) for _, g, c in parts)
        low[span, :] = sum(dot(h, down(c)) for h, _, c in parts)

    front(*steps[0])
    for n, (b, c) in enumerate(steps):
        if n + 1 < len(steps):
            front(*steps[n + 1])
        if c == chunks[-1]:
            products(b)


def feed_kernel(n2, w_up, w_down, hid, slope_ref, low):
    rows, units = hid.shape
    chunk = units // 2
    steps = [(b, c) for b in range(0, rows, QB) for c in range(0, units, chunk)]

    def front(b, c):
        span, cols = slice(b, b + QB), slice(c, c + chunk)
        value, slope = gelu_parts(dot(n2[span, :], w_up[:, cols]))
        hid[span, cols] = value.astype(BF)
        slope_ref[span, cols] = slope.astype(BF)

    front(*steps[0])
    for n, (b, c) in enumerate(steps):
        if n + 1 < len(steps):
            front(*steps[n + 1])
        if c + chunk == units:
            span = slice(b, b + QB)
            low[span, :] = dot(hid[span, :], w_down[...])


def feed_back_kernel(cotr, slope_ref, w_up, w_down, grad, gn_ref):
    rows, units = grad.shape
    chunk = units // 2
    steps = [(b, c) for b in range(0, rows, QB) for c in range(0, units, chunk)]

    def front(b, c):
        span, cols = slice(b, b + QB), slice(c, c + chunk)
        back = dot_nt(cotr[span, :], w_down[cols, :])
        grad[span, cols] = (back * slope_ref[span, cols].astype(F32)).astype(BF)

    front(*steps[0])
    for n, (b, c) in enumerate(steps):
        if n + 1 < len(steps):
            front(*steps[n + 1])
        if c + chunk == units:
            span = slice(b, b + QB)
            gn_ref[span, :] = dot_nt(grad[span, :], w_up[...])


def ffn_oth_kernel(meta, n2, cotr, keep, got, gn_ref, low, hid, grad, w_up, w_down):
    for core, (up_ref, down_ref) in enumerate(((keep, got), (got, keep))):

        @pl.when(meta[2] == core)
        def _():
            w_up[...] = up_ref[...]
            w_down[...] = down_ref[...]

    chunk = hid.shape[1] // 2

    def up(c):
        return w_up[:, c * chunk : (c + 1) * chunk]

    def down(c):
        return w_down[:, c * chunk : (c + 1) * chunk]

    feed_forward(n2, cotr, up, down, hid, grad, gn_ref, low)


def output_kernel(meta, low_a, low_b, oth_a, oth_b, mid_ref, out_ref, wide):
    total = mid_ref.shape[0]
    half = total // 2
    for n, (low, oth) in enumerate(((low_a, oth_a), (low_b, oth_b))):
        for b in range(0, half, QB):
            span = slice(b, b + QB)
            rows = slice(n * half + b, n * half + b + QB)
            put_rows(wide, n * half + b, mid_ref[rows, :] + (low[span, :] + oth[span, :]))
    at = total - meta[0] + meta[1] * half
    for b in range(0, half, QB):
        out_ref[b : b + QB, :] = get_rows(wide, at + b, QB).astype(BF)


def ffn_grads_kernel(
    meta, n2_t, cot_t, hid_a, hid_b, grad_a, grad_b, keep_ref, send_ref
):
    half, chunk = hid_a.shape[0], cot_t.shape[0]
    for core in range(2):

        @pl.when(meta[2] == core)
        def _():
            up_ref, down_ref = (keep_ref, send_ref) if core == 0 else (send_ref, keep_ref)
            for c in range(0, hid_a.shape[1], chunk):
                cols = slice(c, c + chunk)
                up_ref[:, cols] = (
                    dot(n2_t[:, :half], grad_a[:, cols])
                    + dot(n2_t[:, half:], grad_b[:, cols])
                ).astype(BF)
                down = dot(cot_t[:, :half], hid_a[:, cols]) + dot(
                    cot_t[:, half:], hid_b[:, cols]
                )
                down_ref[:, cols] = down.T.astype(BF)


def flip_kernel(x_ref, out_ref):
    for b in range(0, x_ref.shape[0], QB):
        out_ref[:, b : b + QB] = x_ref[b : b + QB, :].T


def middle_kernel(
    meta, own_a, own_b, oth_a, oth_b, mid_ref, cotr_a, cotr_b, gain_two,
    gm_ref, gm_own, small_ref,
    wide,
):
    total, width = mid_ref.shape
    half = total // 2
    gain_acc = jnp.zeros((1, width), F32)
    for b in range(0, total, QB):
        span = slice(b, b + QB)
        at = slice(b % half, b % half + QB)
        own = (own_a if b < half else own_b)[at, :]
        mid = mid_ref[span, :]
        e = own + (oth_a if b < half else oth_b)[at, :].astype(F32)
        scale = lax.rsqrt(jnp.mean(mid * mid, axis=-1, keepdims=True) + EPS)
        se = gain_two[...] * e
        mean = jnp.mean(se * mid, axis=-1, keepdims=True)
        grad = (cotr_a if b < half else cotr_b)[at, :].astype(F32) + (
            scale * se - mid * (scale * scale * scale * mean)
        )
        gm_ref[span, :] = grad.astype(BF)
        put_rows(wide, b, grad)
        gain_acc = gain_acc + jnp.sum(own * mid * scale, axis=0, keepdims=True)
    small_ref[...] = jnp.broadcast_to(gain_acc, small_ref.shape)
    back = total - meta[0]
    for b in range(0, half, QB):
        gm_own[b : b + QB, :] = get_rows(wide, back + meta[1] * half + b, QB)


def attn_bwd_kernel(
    band,
    gm, wo_ref, q_ref, k_ref, v_ref, ctx_ref, inv_ref, pl_ref, pt_ref,
    dq_ref, dk_ref, dv_ref, go_ref, ds_ref, sum_ref,
    ds_long, ds_tail, do_ref, kt_ref, dq_t, inner_ref, do_all, dkv_ref,
):
    total, long = gm.shape[0], pl_ref.shape[1]
    index = {pair: n for n, pair in enumerate(band)}
    lane = lax.broadcasted_iota(jnp.int32, (total, 2 * HD), 1)
    do = dot_nt(gm[...], wo_ref[...]).astype(BF).astype(F32) * inv_ref[...]
    do = do.astype(BF)
    k_t = k_ref[...].T
    inner_t = (do.astype(F32) * ctx_ref[...].astype(F32)).T
    inner = []
    extra = kt_ref.shape[1] - HD
    marks = lax.broadcasted_iota(jnp.int32, (extra, total), 0)
    marks = marks == lax.broadcasted_iota(jnp.int32, (extra, total), 1) // BLK
    marks = jnp.where(marks, 1.0, 0.0).astype(BF)
    for hh in range(2):
        do_ref[hh] = jnp.where((lane < HD) == (hh == 0), do, jnp.zeros_like(do))
        kt_ref[hh, 0:HD, :] = k_t[hh * HD : (hh + 1) * HD, :]
        kt_ref[hh, HD:, :] = marks
        inner.append(jnp.sum(inner_t[hh * HD : (hh + 1) * HD, :], axis=0, keepdims=True))
    inner_ref[...] = jnp.concatenate(
        [jnp.broadcast_to(rows, (8, total)) for rows in inner], axis=0
    )

    def head(hh, carry):
        rows_of_head = pl.ds(pl.multiple_of(hh * HD, HD), HD)
        row = inner_ref[pl.ds(pl.multiple_of(hh * 8, 8), 8), :][0:1, :]
        for start in range(0, total, QB):
            lo, hi = (0, long) if start < long else (long, total)
            terms, ds_here = (pl_ref, ds_long) if start < long else (pt_ref, ds_tail)
            cols = slice(start - lo, start - lo + QB)
            for j in range(lo, hi, BLK):
                rows = slice(j - lo, j - lo + BLK)
                dp = dot_nt(v_ref[j : j + BLK, :], do_ref[hh, start : start + QB, :])
                ds = terms[hh, rows, cols].astype(F32) * (dp - row[:, start : start + QB])
                ds = ds.astype(BF)
                ds_here[rows, cols] = ds
                for c in range(0, QB, BLK):
                    pair = (j // BLK, (start + c) // BLK)
                    if pair in index:
                        ds_ref[hh, index[pair]] = ds[:, c : c + BLK]
            sums = dot(kt_ref[hh, :, lo:hi], ds_here[:, cols])
            dq_t[rows_of_head, start : start + QB] = sums[0:HD, :]
            sum_ref[hh, :, start : start + QB] = sums[HD:, :]
        for lo, hi, ds_here, terms in (
            (0, long, ds_long, pl_ref), (long, total, ds_tail, pt_ref)
        ):
            dkv_ref[hh, 0, lo:hi, :] = dot(ds_here[...], q_ref[lo:hi, :])
            dkv_ref[hh, 1, lo:hi, :] = dot(terms[hh], do_all[lo:hi, :])
        return carry

    do_all[...] = do
    lax.fori_loop(0, 2, head, 0)
    dq = dq_t[...].T * HD ** (-0.5)
    dk = jnp.where(lane < HD, dkv_ref[0, 0], dkv_ref[1, 0])
    dv = jnp.where(lane < HD, dkv_ref[0, 1], dkv_ref[1, 1])
    dq_ref[...] = dq.astype(BF)
    dk_ref[...] = dk.astype(BF)
    dv_ref[...] = dv.astype(BF)
    go_ref[...] = dot(ctx_ref[...].T, gm[...]).astype(BF)


def grads_kernel(pairs, meta, nx_t, *refs):
    pieces, go_pieces = refs[: 3 * pairs], refs[3 * pairs : 4 * pairs]
    keep_ref, send_ref, dqkv = refs[4 * pairs :]
    rows, local = keep_ref.shape[0], pairs * 2 * HD
    for n, piece in enumerate(pieces):
        dqkv[:, n * BLK : (n + 1) * BLK] = piece[...]
    for core in range(2):

        @pl.when(meta[2] == core)
        def _():
            for out, part in ((send_ref, 1 - core), (keep_ref, core)):
                grad = dot(nx_t[part * rows : (part + 1) * rows, :], dqkv[...])
                out[:, : 3 * local] = grad.astype(BF)
                for n, piece in enumerate(go_pieces):
                    out[n * BLK : (n + 1) * BLK, 3 * local :] = piece[
                        :, part * rows : (part + 1) * rows
                    ]


def normed_kernel(pairs, meta, xr_ref, dqkv, wq, wk, wv, gn_own, gn_send, small_ref, wide):
    total, width = xr_ref.shape
    half, local = total // 2, pairs * 2 * HD
    gain_acc = jnp.zeros((1, width), F32)
    for b in range(0, total, QB):
        span = slice(b, b + QB)
        back = sum(
            dot_nt(dqkv[span, n * local : (n + 1) * local], w[...])
            for n, w in enumerate((wq, wk, wv))
        )
        x = xr_ref[span, :].astype(F32)
        scale = lax.rsqrt(jnp.mean(x * x, axis=-1, keepdims=True) + EPS)
        gain_acc = gain_acc + jnp.sum(back * x * scale, axis=0, keepdims=True)
        put_rows(wide, b, back)
    small_ref[...] = jnp.broadcast_to(gain_acc, small_ref.shape)
    at = total - meta[0]
    for b in range(0, half, QB):
        gn_own[b : b + QB, :] = get_rows(wide, at + meta[1] * half + b, QB)
        gn_send[b : b + QB, :] = get_rows(
            wide, at + (1 - meta[1]) * half + b, QB
        ).astype(BF)


def table_kernel(diagonal, blocks, bkt_ref, ds_ref, sum_ref, out_ref):
    lane = lax.broadcasted_iota(jnp.int32, (8, BLK), 1)
    levels, tiles = BUCKETS // 2, BLK // 8
    beside = (ds_ref.shape[1] - diagonal) // 2

    def counted(wanted, n, hh, sums):
        cells = ds_ref[hh, n].astype(F32).reshape(tiles, 8, BLK)
        bucket = bkt_ref[n].reshape(tiles, 8, BLK)
        return tuple(
            total
            + jnp.sum(jnp.where(bucket[r0:r1] == b, cells[r0:r1], 0.0), axis=0)
            for total, (b, r0, r1) in zip(sums, wanted)
        )

    reach = [b if b < levels // 2 else LIMITS[b - levels // 2] - 1 for b in range(levels - 1)]
    spans = [sum(8 * r + 1 <= n for r in range(tiles)) for n in reach[1:]] + [tiles]
    parts = (
        (0, diagonal, [(b, 0, tiles) for b in range(BUCKETS) if b != levels]),
        (diagonal, beside, [(levels + 1 + n, 0, s) for n, s in enumerate(spans)]),
        (diagonal + beside, beside, [(1 + n, tiles - s, tiles) for n, s in enumerate(spans)]),
    )
    zero = jnp.zeros((8, BLK), F32)

    def head(hh, carry):
        sums = [zero] * BUCKETS
        for first, count, wanted in parts:
            found = lax.fori_loop(
                first,
                first + count,
                lambda n, part, wanted=wanted: counted(wanted, n, hh, part),
                (zero,) * len(wanted),
            )
            for (b, _, _), part in zip(wanted, found):
                sums[b] = sums[b] + part
        for i in range(blocks):
            cols = sum_ref[hh, 0:8, i * BLK : (i + 1) * BLK]
            key_block = lax.broadcasted_iota(jnp.int32, (8, BLK), 0)
            far = (key_block < blocks) & (jnp.abs(key_block - i) > 1)
            for b, side in ((levels - 1, key_block < i), (BUCKETS - 1, key_block > i)):
                sums[b] = sums[b] + jnp.where(far & side, cols, 0.0)
        row = zero
        for b in range(BUCKETS):
            row = jnp.where(lane == b, jnp.sum(sums[b]), row)
        out_ref[hh] = row
        return carry

    lax.fori_loop(0, 2, head, 0)


def final_kernel(
    x_ref, gain, gn_own, gn_oth, gm_ref, grad_ref
):
    for b in range(0, x_ref.shape[0], QB):
        span = slice(b, b + QB)
        x = x_ref[span, :].astype(F32)
        e = gn_own[span, :] + gn_oth[span, :].astype(F32)
        scale = lax.rsqrt(jnp.mean(x * x, axis=-1, keepdims=True) + EPS)
        se = gain[...] * e
        mean = jnp.mean(se * x, axis=-1, keepdims=True)
        grad_ref[span, :] = (
            gm_ref[span, :] + (scale * se - x * (scale * scale * scale * mean))
        ).astype(BF)


def add_kernel(at, meta, keep, got, *outs):
    rows = outs[0].shape[0]
    if len(outs) == 1:
        outs[0][...] = (keep[...].astype(F32) + got[...].astype(F32)).astype(BF)
        return
    for out, part in ((outs[0], meta[at]), (outs[1], 1 - meta[at])):
        span = pl.ds(pl.multiple_of(part * rows, 16), rows)
        out[...] = (keep[span, :].astype(F32) + got[span, :].astype(F32)).astype(BF)


def join_kernel(at, meta, mine, got, out):
    rows = mine.shape[0]
    out[pl.ds(pl.multiple_of(meta[at] * rows, 16), rows), :] = mine[...]
    out[pl.ds(pl.multiple_of((1 - meta[at]) * rows, 16), rows), :] = got[...]


def little_kernel(a_ref, b_ref, out_ref):
    out_ref[...] = a_ref[...] + b_ref[...]


def split_ffn_kernel(meta, mine, got, up_ref, down_ref):
    width = down_ref.shape[1]
    for core in range(2):

        @pl.when(meta[2] == core)
        def _():
            up, down = (mine, got) if core == 0 else (got, mine)
            up_ref[...] = up[...].astype(F32)
            for n in range(down.shape[1] // width):
                rows = slice(n * down.shape[0], (n + 1) * down.shape[0])
                down_ref[rows, :] = down[:, n * width : (n + 1) * width].astype(F32)


def split_attn_kernel(meta, mine, got, q_ref, k_ref, v_ref, o_ref):
    rows, local = mine.shape[0], q_ref.shape[1]
    for core in range(2):

        @pl.when(meta[2] == core)
        def _():
            for n, part in enumerate((mine, got) if core == 0 else (got, mine)):
                span = slice(n * rows, (n + 1) * rows)
                for m, out in enumerate((q_ref, k_ref, v_ref)):
                    out[span, :] = part[:, m * local : (m + 1) * local].astype(F32)
                o_ref[:, span] = part[:, 3 * local :].astype(F32)


def swap(value, size, flip, axis="dp"):
    return lax.ppermute(value, axis, [(n, flip(n)) for n in range(size)])


class Exchange:
    def __init__(self, name, meta, size, orders):
        self.name, self.meta, self.size, self.orders = name, meta, size, orders
        self.phase, self.joins, self.waiting = -1, [], -2

    def gather(self, piece, cuts):
        self.keep, self.joins = piece, list(range(cuts))
        self.back()
        return self

    def sum(self, keep, send):
        self.keep = keep
        self.got = swap(send, self.size, lambda n: n ^ 1)
        return self

    def flip(self, phase):
        if phase < 0:
            return lambda n: n ^ 1
        orders = self.orders
        return lambda n: n ^ (1 << orders[n & 1][phase])

    def pair(self, value):
        return (value, full(value.shape))

    def reduce(self, after=()):
        self.phase += 1
        shape = self.keep.shape
        last = self.phase == len(self.orders[0])
        cut = not last and shape[0] % 32 == 0
        rows = shape[0] // 2 if cut else shape[0]
        out = (jax.ShapeDtypeStruct((rows, shape[1]), BF), full((rows, shape[1])))
        parts = call(
            functools.partial(add_kernel, 3 + self.phase),
            [(self.meta, smem()), self.pair(self.keep), self.pair(self.got)],
            [out, out] if cut else [out],
            name=f"{self.name}_add{self.phase}",
            after=after,
        )
        self.keep = parts[0]
        if last:
            self.back()
            return self.keep
        if cut:
            self.joins.append(self.phase)
        self.got = swap(parts[-1], self.size, self.flip(self.phase))
        return self.keep

    def back(self, parts=1):
        phase = self.joins.pop() if self.joins else -1
        self.waiting = phase
        if phase < 0 and parts > 1:
            self.got = [
                swap(v, self.size, self.flip(phase))
                for v in jnp.split(self.keep, parts, axis=1)
            ]
            return
        self.got = swap(self.keep, self.size, self.flip(phase))

    def join(self, after=(), parts=1):
        rows, cols = self.keep.shape
        self.keep = call(
            functools.partial(join_kernel, 3 + self.waiting),
            [(self.meta, smem()), self.pair(self.keep), self.pair(self.got)],
            [(jax.ShapeDtypeStruct((2 * rows, cols), BF), full((2 * rows, cols)))],
            name=f"{self.name}_join{self.waiting}",
            after=after,
        )[0]
        self.back(parts)
        return self.keep


def body(
    inputs, norm_one, w_query, w_key, w_value, w_out, bias_table, norm_two, w_up, w_down,
    doc_lengths, layout_steps, cotangent, *, size,
):
    row_len = layout_steps.shape[0]
    half, width = inputs.shape
    long = 3 * row_len // 4
    local = w_query.shape[1]
    pairs = local // (2 * HD)
    hidden_units = w_up.shape[1]
    mp = lax.axis_index("mp")
    dp = lax.axis_index("dp")
    core = dp & 1
    band = band_blocks(long // BLK, row_len // BLK)
    count = len(band)

    def other(value):
        return swap(value, 2, lambda n: 1 - n, "mp")

    def core_swap(value):
        return swap(value, size, lambda n: n ^ 1)

    doc_ends = jnp.cumsum(doc_lengths[0])
    turn = jnp.sum(
        jnp.where(doc_lengths[0] == long, doc_ends - doc_lengths[0], 0)
    ).astype(jnp.int32)
    places = jnp.arange(row_len, dtype=jnp.int32)
    segment = jnp.sum((places[:, None] >= doc_ends[None, :]).astype(jnp.int32), axis=1)
    position = jnp.cumsum(layout_steps)
    both = jnp.stack([position, segment])
    both = lax.dynamic_slice_in_dim(
        jnp.concatenate([both, both], axis=1), turn, row_len, 1
    ).astype(jnp.int32)

    table = jnp.pad(bias_table.T, ((0, 8 - bias_table.shape[1]), (0, 0)))
    table = jnp.concatenate(
        [table, jnp.full((8, BLK - BUCKETS), MASKED, F32)], axis=1
    )
    gain_one, gain_two = norm_one.reshape(1, width), norm_two.reshape(1, width)

    depth = size.bit_length() - 1
    rest = list(range(1, depth))
    orders = (rest, rest[1:] + rest[:1])
    bits = [(dp >> b) & 1 for b in range(depth)]
    phase_bits = [
        jnp.where(core == 0, bits[orders[0][t]], bits[orders[1][t]])
        for t in range(depth - 1)
    ]
    meta = jnp.stack([turn, mp, core] + phase_bits).astype(jnp.int32)

    shape = jax.ShapeDtypeStruct
    heads = 2 * pairs
    tail = row_len - long
    part = width // 2
    pair_block = pl.BlockSpec((row_len, 2 * HD), lambda p: (0, p))
    weight_block = pl.BlockSpec((width, 2 * HD), lambda p: (0, p))

    def whole(value):
        return (value, full(value.shape))

    def out(dims, kind=BF, spec=None):
        return (shape(dims, kind), spec or full(dims))

    def cuts_of(rows):
        cuts = 0
        while cuts < depth - 1 and rows % 32 == 0:
            rows, cuts = rows // 2, cuts + 1
        return cuts, rows

    def piece_of(rows):
        cuts, least = cuts_of(rows)
        return sum(phase_bits[t] * (rows // least >> (t + 1)) for t in range(cuts))

    ffn_cuts, ffn_rows = cuts_of(width)
    at = jnp.stack([piece_of(width), core]).astype(jnp.int32)
    anywhere = pl.BlockSpec(memory_space=pl.ANY)
    x_oth = other(inputs)
    early = 3 * half // 8
    ffn_piece, wo_send, cot_a = call(
        pieces_kernel,
        [
            (at, smem()), (w_out, anywhere), (w_up, anywhere), (w_down, anywhere),
            (cotangent, anywhere),
        ],
        [out((ffn_rows, hidden_units)), out((local, part)), out((early, width))],
        name="pieces",
        scratch=[pltpu.SemaphoreType.DMA((4,))],
        limit=VMEM_LIMIT,
        after=[both, meta, table, gain_one, gain_two],
    )
    ffn_piece = other(ffn_piece)
    wo_a = other(wo_send)
    cot_a = other(cot_a)

    work = [
        pltpu.VMEM((2, long, QB), F32),
        pltpu.VMEM((2, HD + 16, row_len), BF),
        pltpu.VMEM((2, row_len, 2 * HD), BF),
        pltpu.VMEM((row_len, 2 * HD), BF),
        pltpu.VMEM((2 * HD, row_len), F32),
    ]
    wide = pltpu.VMEM((width // BLK, 2 * row_len, BLK), F32)
    long_spec = pl.BlockSpec((2, long, long), lambda p: (p, 0, 0))
    tail_spec = pl.BlockSpec((2, tail, tail), lambda p: (p, 0, 0))
    xr, nx, qs, keys, values, ctx_own, inv, p_long, p_tail, bkt = call(
        functools.partial(attn_own_kernel, long, band),
        [
            (meta, smem()), whole(inputs), whole(x_oth), whole(gain_one), whole(both),
            (w_query, weight_block), (w_key, weight_block), (w_value, weight_block),
            whole(table),
        ],
        [
            out((row_len, width)), out((row_len, width)),
            out((row_len, local), BF, pair_block), out((row_len, local), BF, pair_block),
            out((row_len, local), BF, pair_block), out((row_len, local), BF, pair_block),
            out((row_len, local), F32, pair_block), out((heads, long, long), BF, long_spec),
            out((heads, tail, tail), BF, tail_spec), out((count, BLK, BLK), jnp.int32),
        ],
        name="attend_own",
        grid=(pairs,),
        scratch=[wide] + work + [pltpu.VMEM((2 * HD, row_len), F32)],
    )

    ctx_send, ffn_piece, wo_a, cot_a = call(
        copy_kernel,
        [whole(v) for v in (ctx_own, ffn_piece, wo_a, cot_a)],
        [out(v.shape) for v in (ctx_own, ffn_piece, wo_a, cot_a)],
        name="take_pieces",
    )
    ctx_oth = other(ctx_send)
    (cot_send,) = call(
        copy_kernel, [whole(cotangent[early:])], [out((half - early, width))],
        name="take_cotangent", after=[ctx_send],
    )
    cot_b = other(cot_send)
    ffn_w = Exchange("ffn_w", meta, size, orders).gather(ffn_piece, ffn_cuts)
    wo_b = core_swap(wo_a)
    mark = wo_b
    if ffn_w.waiting >= 0:
        mark = ffn_w.join([wo_b])

    mid, n2_a, n2_b, n2_t = call(
        join_heads_kernel,
        [
            (meta, smem()), whole(xr), whole(ctx_own), whole(ctx_oth), whole(w_out),
            whole(wo_a), whole(wo_b), whole(gain_two),
        ],
        [
            out((row_len, width), F32), out((half, width)), out((half, width)),
            out((width, row_len)),
        ],
        name="join_heads",
        after=[mark],
    )
    n2 = (n2_a, n2_b)
    mark = n2_b
    hid, slopes, low = [], [], []
    for h in range(2):
        hid_h, slope_h, low_h = call(
            feed_kernel,
            [whole(n2[h]), whole(w_up), whole(w_down)],
            [out((half, hidden_units)), out((half, hidden_units)), out((half, width), F32)],
            name=f"feed{h}",
            after=[mark],
        )
        mark = low_h
        hid.append(hid_h)
        slopes.append(slope_h)
        low.append(low_h)
    *cotr, cot_t = call(
        turn_kernel,
        [(meta, smem()), whole(cotangent), whole(cot_a), whole(cot_b)],
        [out((half, width)), out((half, width)), out((width, row_len))],
        name="turn_cotangent",
        scratch=[wide],
        after=[mark],
    )
    mark = cot_t
    if ffn_w.waiting >= 0 and ffn_w.joins:
        mark = ffn_w.join([mark])
    grad_pre, gn2_own, gn2_oth, low_oth = [], [], [], []
    for h in range(2):
        grad_h, own_h = call(
            feed_back_kernel,
            [whole(cotr[h]), whole(slopes[h]), whole(w_up), whole(w_down)],
            [out((half, hidden_units)), out((half, width), F32)],
            name=f"feed_back{h}",
            after=[mark],
        )
        mark = own_h
        grad_pre.append(grad_h)
        gn2_own.append(own_h)
    ffn_keep, ffn_send = call(
        ffn_grads_kernel,
        [(meta, smem()), whole(n2_t), whole(cot_t)] + [whole(v) for v in hid + grad_pre],
        [out((width, hidden_units)), out((width, hidden_units))],
        name="ffn_grads",
        after=[mark],
    )
    ffn = Exchange("ffn", meta, size, orders).sum(ffn_keep, ffn_send)
    mark = ffn_keep
    while ffn_w.waiting >= 0:
        mark = ffn_w.join([mark])
    mark = ffn.reduce([mark])
    for h in range(2):
        oth_h, low_h = call(
            ffn_oth_kernel,
            [
                (meta, smem()), whole(n2[h]), whole(cotr[h]), whole(ffn_w.keep),
                whole(ffn_w.got),
            ],
            [out((half, width), F32), out((half, width), F32)],
            name=f"feed_oth{h}",
            scratch=[
                pltpu.VMEM((half, hidden_units), BF),
                pltpu.VMEM((half, hidden_units), BF),
                pltpu.VMEM((width, hidden_units), BF),
                pltpu.VMEM((width, hidden_units), BF),
            ],
            after=[mark],
        )
        mark = low_h
        gn2_oth.append(oth_h)
        low_oth.append(low_h)
    mark = mark_one = ffn.reduce([mark])
    (nx_t,) = call(
        flip_kernel, [whole(nx)], [out((width, row_len))], name="flip", after=[mark]
    )

    gm, gm_own, small_two = call(
        middle_kernel,
        [(meta, smem())]
        + [whole(v) for v in gn2_own + gn2_oth]
        + [whole(mid)]
        + [whole(v) for v in cotr]
        + [whole(gain_two)],
        [out((row_len, width)), out((half, width), F32), out((8, width), F32)],
        name="grad_middle",
        scratch=[wide],
        after=[nx_t],
    )
    tables = []

    def table_sums(p, after):
        (sums,) = call(
            functools.partial(table_kernel, row_len // BLK, long // BLK),
            [whole(bkt), whole(ds_pieces[p]), whole(sum_pieces[p])],
            [out((2, 8, BLK), F32)],
            name=f"table_sums{p}",
            after=after,
        )
        tables.append(sums)
        return sums

    pieces, go_pieces, ds_pieces, sum_pieces = [], [], [], []
    for p in range(pairs):
        pair = pl.BlockSpec((row_len, 2 * HD), lambda *_, p=p: (0, p))
        dq, dk, dv, go, ds, sums = call(
            functools.partial(attn_bwd_kernel, band),
            [
                whole(gm), (w_out, pl.BlockSpec((2 * HD, width), lambda *_, p=p: (p, 0))),
                (qs, pair), (keys, pair), (values, pair), (ctx_own, pair), (inv, pair),
                (p_long, pl.BlockSpec((2, long, long), lambda *_, p=p: (p, 0, 0))),
                (p_tail, pl.BlockSpec((2, tail, tail), lambda *_, p=p: (p, 0, 0))),
            ],
            [
                out((row_len, 2 * HD)), out((row_len, 2 * HD)), out((row_len, 2 * HD)),
                out((2 * HD, width)), out((2, count, BLK, BLK)), out((2, 16, row_len), F32),
            ],
            name=f"attend_back{p}",
            scratch=[
                pltpu.VMEM((long, long), BF),
                pltpu.VMEM((tail, tail), BF),
                pltpu.VMEM((2, row_len, 2 * HD), BF),
                pltpu.VMEM((2, HD + 16, row_len), BF),
                pltpu.VMEM((2 * HD, row_len), F32),
                pltpu.VMEM((16, row_len), F32),
                pltpu.VMEM((row_len, 2 * HD), BF),
                pltpu.VMEM((2, 2, row_len, 2 * HD), F32),
            ],
            after=[mark],
        )
        pieces.append((dq, dk, dv))
        go_pieces.append(go)
        ds_pieces.append(ds)
        sum_pieces.append(sums)
        mark = dq
        if p == 1:
            for _ in range(depth - 3):
                mark = ffn.reduce([mark])
    mark = table_sums(0, [mark])
    mark = ffn.reduce([mark])
    operands = [whole(pieces[p][n]) for n in range(3) for p in range(pairs)]
    attn_keep, attn_send, dqkv = call(
        functools.partial(grads_kernel, pairs),
        [(meta, smem()), whole(nx_t)] + operands + [whole(go) for go in go_pieces],
        [
            out((part, 3 * local + part)), out((part, 3 * local + part)),
            out((row_len, 3 * local)),
        ],
        name="attend_grads",
        after=[mark],
    )
    attn = Exchange("attn", meta, size, orders).sum(attn_keep, attn_send)
    gn_own, gn_send, small_one = call(
        functools.partial(normed_kernel, pairs),
        [
            (meta, smem()), whole(xr), whole(dqkv), whole(w_query), whole(w_key),
            whole(w_value),
        ],
        [out((half, width), F32), out((half, width)), out((8, width), F32)],
        name="grad_normed",
        scratch=[wide],
    )
    gn_oth = other(gn_send)
    gains = jnp.concatenate([small_one[0:1], small_two[0:1]], axis=0)
    gains = gains.reshape(2 * width // BLK, BLK)
    gains_oth = other(gains)

    def join_ffn(after):
        return ffn.join([after]) if ffn.waiting >= 0 else after

    mark = attn.reduce([small_one])
    mark = table_sums(1, [mark])
    mark = join_ffn(mark)
    mark = attn.reduce([mark])
    for p in range(2, pairs):
        mark = table_sums(p, [mark])
    little = jnp.concatenate([gains + gains_oth] + [t[:, 0, :] for t in tables], axis=0)
    got, phase = swap(little, size, attn.flip(0)), 0

    def little_step(after):
        nonlocal little, got, phase
        little = call(
            little_kernel,
            [whole(little), whole(got)],
            [out(little.shape, F32)],
            name=f"little{phase}",
            after=[after],
        )[0]
        phase += 1
        if phase < depth:
            got = swap(little, size, attn.flip(phase if phase < depth - 1 else -1))
        return little

    while attn.phase < depth - 2:
        mark = attn.reduce([mark, gains_oth])
    mark = little_step(mark)
    mark = attn.reduce([mark, gn_oth])
    mark = little_step(mark)
    mark = join_ffn(mark)
    mark = attn.join([mark]) if attn.waiting >= 0 else mark
    (output,) = call(
        output_kernel,
        [(meta, smem())] + [whole(v) for v in low + low_oth] + [whole(mid)],
        [out((half, width))],
        name="output",
        scratch=[wide],
        limit=VMEM_LIMIT,
        after=[mark],
    )
    mark = output
    while phase < depth - 1:
        mark = little_step(mark)
    while attn.waiting > 0:
        mark = attn.join([mark])
    while ffn.waiting >= 0:
        mark = ffn.join([mark])
    (input_grad,) = call(
        final_kernel,
        [
            whole(inputs), whole(gain_one), whole(gn_own), whole(gn_oth), whole(gm_own),
        ],
        [out((half, width))],
        name="input_grad",
        after=[mark],
    )
    grad_up, grad_down = call(
        split_ffn_kernel,
        [(meta, smem()), whole(ffn.keep), whole(ffn.got)],
        [out((width, hidden_units), F32), out((hidden_units, width), F32)],
        name="ffn_split",
        after=[input_grad],
    )
    mark = grad_up
    if attn.waiting >= 0:
        mark = attn.join([mark])
    little_step(mark)
    grad_query, grad_key, grad_value, grad_out = call(
        split_attn_kernel,
        [(meta, smem()), whole(attn.keep), whole(attn.got)],
        [
            out((width, local), F32), out((width, local), F32), out((width, local), F32),
            out((local, width), F32),
        ],
        name="attn_split",
    )
    gains = little[: 2 * width // BLK].reshape(2, width)
    grad_table = little[2 * width // BLK :, :BUCKETS].T
    return (
        output, input_grad, gains[0], gains[1], grad_query, grad_key, grad_value,
        grad_out, grad_table, grad_up, grad_down,
    )


def solution(mesh):
    placed = (
        P(("dp", "mp"), None),
        P(),
        P(None, "mp"),
        P(None, "mp"),
        P(None, "mp"),
        P("mp", None),
        P(None, "mp"),
        P(),
        P(None, "mp"),
        P("mp", None),
        P("dp", None),
        P("dp"),
        P(("dp", "mp"), None),
    )
    return jax.shard_map(
        functools.partial(body, size=mesh.shape["dp"]),
        mesh=mesh,
        in_specs=placed,
        out_specs=(
            P(("dp", "mp"), None),
            P(("dp", "mp"), None),
            P(),
            P(),
            P(None, "mp"),
            P(None, "mp"),
            P(None, "mp"),
            P("mp", None),
            P(None, "mp"),
            P(None, "mp"),
            P("mp", None),
        ),
        check_vma=False,
    )
```

```python
import functools

import jax
import jax.numpy as jnp
from jax import lax
from jax.experimental import pallas as pl
from jax.experimental.pallas import tpu as pltpu
from jax.sharding import PartitionSpec as P

HD = 64
BUCKETS = 32
MAX_DIST = 128
EPS = 1e-06
MASKED = -1000000000.0
BLK = 128
QB = 256
CUT = 64
GELU_C = 0.7978845608028654
GELU_A = 0.044715
BF = jnp.bfloat16
F32 = jnp.float32
VMEM_LIMIT = 56 * 1024 * 1024
SPARE = 4 * 1024 * 1024


def bucket_limits(buckets, reach):
    halfway = buckets // 2
    exact_span = halfway // 2
    levels = halfway - exact_span
    limits = []
    for degree in range(1, levels):
        target = exact_span ** (levels - degree) * reach**degree
        candidate = exact_span
        while candidate**levels < target:
            candidate = candidate + 1
        limits.append(candidate)
    return limits


LIMITS = bucket_limits(BUCKETS, MAX_DIST)


def dot(a, b):
    return jnp.dot(a, b, preferred_element_type=F32)


def dot_nt(a, b):
    return lax.dot_general(a, b, (((1,), (1,)), ((), ())), preferred_element_type=F32)


def band_blocks(long_blocks, blocks):
    steps = [n for n in range(blocks - 1) if n + 1 != long_blocks]
    return (
        [(n, n) for n in range(blocks)]
        + [(n + 1, n) for n in steps]
        + [(n, n + 1) for n in steps]
    )


def nbytes(shape, kind):
    if isinstance(kind, jax.ShapeDtypeStruct):
        kind = kind.dtype
    rows = -(-shape[-2] // 16) * 16 if len(shape) > 1 else 8
    lanes = -(-shape[-1] // BLK) * BLK
    lead = 1
    for n in shape[:-2]:
        lead = lead * n
    return lead * rows * lanes * jnp.dtype(kind).itemsize


def call(kernel, operands, outs, *, name, grid=(), scratch=(), after=(), limit=None):
    count = len(operands)

    def run(*refs):
        kernel(*refs[:count], *refs[count + len(after) :])

    arrays = list(operands) + list(outs)
    if not grid and any(
        s.block_shape is not None and tuple(s.block_shape) != v.shape for v, s in arrays
    ):
        grid = (1,)
    need = sum(nbytes(s.shape, s.dtype) for s in scratch if len(s.shape) > 1)
    for value, spec in arrays:
        if spec.block_shape is not None:
            need += (2 if grid else 1) * nbytes(spec.block_shape, value.dtype)
    limit = limit or min(VMEM_LIMIT, need + (need >> 3) + SPARE)
    return pl.pallas_call(
        run,
        grid=grid,
        in_specs=[spec for _, spec in operands]
        + [pl.BlockSpec(memory_space=pl.ANY)] * len(after),
        out_specs=[spec for _, spec in outs],
        out_shape=[kind for kind, _ in outs],
        scratch_shapes=list(scratch),
        compiler_params=pltpu.CompilerParams(
            vmem_limit_bytes=limit, dimension_semantics=("arbitrary",) * len(grid)
        ),
        cost_estimate=pl.CostEstimate(
            flops=1, bytes_accessed=1, transcendentals=0
        ),
        name=name,
    )(*[array for array, _ in operands], *after)


def full(shape):
    return pl.BlockSpec(shape, lambda *_: (0,) * len(shape))


def smem():
    return pl.BlockSpec(memory_space=pltpu.SMEM)


def put_rows(wide, row, value):
    total = wide.shape[1] // 2
    count = value.shape[0]
    for n in range(wide.shape[0]):
        cols = value[:, n * BLK : (n + 1) * BLK]
        wide[n, pl.ds(row, count), :] = cols
        wide[n, pl.ds(row + total, count), :] = cols


def get_rows(wide, row, count):
    return jnp.concatenate(
        [wide[n, pl.ds(row, count), :] for n in range(wide.shape[0])], axis=1
    )


def put_halves(wide, own_ref, oth_refs, mp):
    half = own_ref.shape[0]
    for side, refs in ((mp, [own_ref]), (1 - mp, oth_refs)):
        at = 0
        for ref in refs:
            for b in range(0, ref.shape[0], CUT):
                rows = ref[b : b + CUT, :].astype(F32)
                put_rows(wide, pl.multiple_of(side * half + at + b, CUT), rows)
            at += ref.shape[0]


def write_buckets(bkt_ref, posc, posr, segc, segr, band, long_blocks):
    for n, (j, i) in enumerate(band):
        rows, cols = slice(j * BLK, (j + 1) * BLK), slice(i * BLK, (i + 1) * BLK)
        offset = posc[rows, :] - posr[:, cols]
        distance = jnp.abs(offset)
        bucket = jnp.where(offset > 0, BUCKETS // 2, 0) + jnp.minimum(
            distance, BUCKETS // 4
        )
        for limit in LIMITS:
            bucket = bucket + jnp.where(distance >= limit, 1, 0)
        if j >= long_blocks:
            bucket = jnp.where(segc[rows, :] == segr[:, cols], bucket, BUCKETS)
        bkt_ref[n] = bucket


def attend_pair(p, qs, k, v_t, tab_ref, bkt_ref, p_long, p_tail, work, band):
    scores, values, queries, k_ref, ctx_t, inv_t = work
    long, total = p_long.shape[1], ctx_t.shape[1]
    index = {pair: n for n, pair in enumerate(band)}
    lane = lax.broadcasted_iota(jnp.int32, (total, 2 * HD), 1)
    k_ref[...] = k
    tables = []
    for hh in range(2):
        values[hh, 0:HD, :] = v_t[hh * HD : (hh + 1) * HD, :]
        values[hh, HD:, :] = jnp.ones((values.shape[1] - HD, total), BF)
        queries[hh] = jnp.where((lane < HD) == (hh == 0), qs, jnp.zeros_like(qs))
        row = tab_ref[pl.ds(2 * p + hh, 1), :]
        tables.append(
            (
                jnp.broadcast_to(row, (BLK, BLK)),
                row[:, BUCKETS // 2 - 1 : BUCKETS // 2],
                row[:, BUCKETS - 1 : BUCKETS],
            )
        )
    units = [(hh, start) for hh in range(2) for start in range(0, total, QB)]
    tops = {}

    def span(u):
        return (0, long) if units[u][1] < long else (long, total)

    def score(u, j):
        hh, start = units[u]
        lo = span(u)[0]
        table, behind, ahead = tables[hh]
        cells = dot_nt(k_ref[j : j + BLK, :], queries[hh, start : start + QB, :])
        tops_here = []
        for c in range(0, QB, BLK):
            pair = (j // BLK, (start + c) // BLK)
            if pair in index:
                bias = jnp.take_along_axis(
                    table, bkt_ref[index[pair]], axis=1, mode="promise_in_bounds"
                )
            else:
                bias = ahead if pair[0] > pair[1] else behind
            cell = cells[:, c : c + BLK] + bias
            scores[u % 2, j - lo : j - lo + BLK, c : c + BLK] = cell
            tops_here.append(jnp.max(cell.reshape(BLK // 8, 8, BLK), axis=0))
        top = jnp.concatenate(tops_here, axis=1)
        tops[u] = jnp.maximum(tops[u], top) if u in tops else top

    def term(u, j):
        hh, start = units[u]
        lo = span(u)[0]
        out = p_long if start < long else p_tail
        if j == lo:
            tops[u] = jnp.max(tops[u], axis=0, keepdims=True)
        terms = jnp.exp(scores[u % 2, j - lo : j - lo + BLK, :] - tops[u])
        out[hh, j - lo : j - lo + BLK, start - lo : start - lo + QB] = terms.astype(BF)

    def context(u):
        hh, start = units[u]
        lo, hi = span(u)
        out = p_long if start < long else p_tail
        sums = dot(values[hh, :, lo:hi], out[hh, :, start - lo : start - lo + QB])
        inverse = 1.0 / sums[HD : HD + 1, :]
        rows, cols = slice(hh * HD, (hh + 1) * HD), slice(start, start + QB)
        ctx_t[rows, cols] = sums[0:HD, :] * inverse
        if inv_t is not None:
            inv_t[rows, cols] = jnp.broadcast_to(inverse, (HD, QB))

    for j in range(*span(0), BLK):
        score(0, j)
    for u in range(len(units)):
        ahead_of = list(range(*span(u + 1), BLK)) if u + 1 < len(units) else []
        here = list(range(*span(u), BLK))
        for n in range(max(len(ahead_of), len(here))):
            if n < len(ahead_of):
                score(u + 1, ahead_of[n])
            if n < len(here):
                term(u, here[n])
        context(u)


def pieces_kernel(at, wo, up, down, cot, ffn_ref, out_ref, cot_ref, sems):
    rows, width = ffn_ref.shape[0], down.shape[1]
    part = out_ref.shape[1]
    start = pl.multiple_of(at[0] * rows, 16)
    first = pltpu.make_async_copy(
        wo.at[:, pl.ds(pl.multiple_of(at[1] * part, BLK), part)], out_ref, sems.at[0]
    )
    first.start()
    rows_of_cot = pltpu.make_async_copy(
        cot.at[0 : cot_ref.shape[0], :], cot_ref, sems.at[3]
    )
    rows_of_cot.start()

    @pl.when(at[1] == 0)
    def _():
        copy = pltpu.make_async_copy(up.at[pl.ds(start, rows), :], ffn_ref, sems.at[1])
        copy.start()
        copy.wait()

    @pl.when(at[1] == 1)
    def _():
        copies = [
            pltpu.make_async_copy(
                down.at[pl.ds(n * width + start, rows), :],
                ffn_ref.at[:, n * width : (n + 1) * width],
                sems.at[1 + n],
            )
            for n in range(2)
        ]
        for copy in copies:
            copy.start()
        for copy in copies:
            copy.wait()

    first.wait()
    rows_of_cot.wait()


def copy_kernel(*refs):
    for x_ref, out_ref in zip(refs[: len(refs) // 2], refs[len(refs) // 2 :]):
        out_ref[...] = x_ref[...]


def attn_own_kernel(
    long, band,
    meta, x_own, x_oth, gain, place_ref, wq, wk, wv, tab,
    xr_ref, nx_ref, q_ref, k_ref, v_ref, ctx_ref, inv_ref, pl_ref, pt_ref, bkt_ref,
    wide, scores, vals, queries, keys, ctx_t, inv_t,
):
    p = pl.program_id(0)
    total = xr_ref.shape[0]

    @pl.when(p == 0)
    def _():
        put_halves(wide, x_own, [x_oth], meta[1])
        for b in range(0, total, QB):
            rows = get_rows(wide, meta[0] + b, QB)
            xr_ref[b : b + QB, :] = rows.astype(BF)
            scale = lax.rsqrt(jnp.mean(rows * rows, axis=-1, keepdims=True) + EPS)
            nx_ref[b : b + QB, :] = (rows * scale * gain[...]).astype(BF)
        places = place_ref[...].astype(F32)
        down = [
            jnp.broadcast_to(places[n : n + 1, :], (BLK, total)).T.astype(jnp.int32)
            for n in range(2)
        ]
        write_buckets(
            bkt_ref, down[0], place_ref[0:1, :], down[1], place_ref[1:2, :], band,
            long // BLK,
        )

    nx = nx_ref[...]
    qs = (dot(nx, wq[...]).astype(BF).astype(F32) * HD ** (-0.5)).astype(BF)
    k = dot(nx, wk[...]).astype(BF)
    v = dot(nx, wv[...]).astype(BF)
    q_ref[...] = qs
    k_ref[...] = k
    v_ref[...] = v
    work = (scores, vals, queries, keys, ctx_t, inv_t)
    attend_pair(p, qs, k, v.T, tab, bkt_ref, pl_ref, pt_ref, work, band)
    ctx_ref[...] = ctx_t[...].T.astype(BF)
    inv_ref[...] = inv_t[...].T


def join_heads_kernel(
    meta, xr_ref, ctx_own, ctx_oth, wo_own, wo_a, wo_b, gain, mid_ref, n2_a, n2_b, n2_t,
):
    total, width = xr_ref.shape
    half = total // 2
    part = width // 2
    for b in range(0, total, QB):
        span = slice(b, b + QB)
        mid_ref[span, :] = xr_ref[span, :].astype(F32) + dot(
            ctx_own[span, :], wo_own[...]
        )
        for piece, core in ((wo_a, meta[2]), (wo_b, 1 - meta[2])):
            cols = pl.ds(pl.multiple_of(core * part, BLK), part)
            mid_ref[span, cols] += dot(ctx_oth[span, :], piece[...])
        mid = mid_ref[span, :]
        scale = lax.rsqrt(jnp.mean(mid * mid, axis=-1, keepdims=True) + EPS)
        rows = (mid * scale * gain[...]).astype(BF)
        (n2_a if b < half else n2_b)[b % half : b % half + QB, :] = rows
        n2_t[:, span] = rows.T


def turn_kernel(meta, own_ref, oth_a, oth_b, out_a, out_b, out_t, wide):
    half = out_a.shape[0]
    total = 2 * half
    put_halves(wide, own_ref, [oth_a, oth_b], meta[1])
    for b in range(0, total, QB):
        rows = get_rows(wide, meta[0] + b, QB).astype(BF)
        (out_a if b < half else out_b)[b % half : b % half + QB, :] = rows
        out_t[:, b : b + QB] = rows.T


def gelu_parts(pre):
    square = pre * pre
    tanh = jnp.tanh(pre * (GELU_C + GELU_C * GELU_A * square))
    gate = 0.5 + 0.5 * tanh
    slope = gate + pre * (0.5 - 0.5 * tanh * tanh) * (
        GELU_C + 3.0 * GELU_C * GELU_A * square
    )
    return pre * gate, slope


def feed_forward(n2, cotr, up, down, hid, grad, gn_ref, low):
    rows, units = hid.shape
    chunk = up(0).shape[1]
    chunks = range(units // chunk)
    steps = [(b, c) for b in range(0, rows, QB) for c in chunks]

    def front(b, c):
        span, cols = slice(b, b + QB), slice(c * chunk, (c + 1) * chunk)
        value, slope = gelu_parts(dot(n2[span, :], up(c)))
        back = dot_nt(cotr[span, :], down(c))
        hid[span, cols] = value.astype(BF)
        grad[span, cols] = (back * slope).astype(BF)

    def products(b):
        span = slice(b, b + QB)
        parts = [(hid[span, c * chunk : (c + 1) * chunk],
                  grad[span, c * chunk : (c + 1) * chunk], c) for c in chunks]
        gn_ref[span, :] = sum(dot_nt(g, up(c)) for _, g, c in parts)
        low[span, :] = sum(dot(h, down(c)) for h, _, c in parts)

    front(*steps[0])
    for n, (b, c) in enumerate(steps):
        if n + 1 < len(steps):
            front(*steps[n + 1])
        if c == chunks[-1]:
            products(b)


def feed_kernel(n2, w_up, w_down, hid, slope_ref, low):
    rows, units = hid.shape
    chunk = units // 2
    steps = [(b, c) for b in range(0, rows, QB) for c in range(0, units, chunk)]

    def front(b, c):
        span, cols = slice(b, b + QB), slice(c, c + chunk)
        value, slope = gelu_parts(dot(n2[span, :], w_up[:, cols]))
        hid[span, cols] = value.astype(BF)
        slope_ref[span, cols] = slope.astype(BF)

    front(*steps[0])
    for n, (b, c) in enumerate(steps):
        if n + 1 < len(steps):
            front(*steps[n + 1])
        if c + chunk == units:
            span = slice(b, b + QB)
            low[span, :] = dot(hid[span, :], w_down[...])


def feed_back_kernel(cotr, slope_ref, w_up, w_down, grad, gn_ref):
    rows, units = grad.shape
    chunk = units // 2
    steps = [(b, c) for b in range(0, rows, QB) for c in range(0, units, chunk)]

    def front(b, c):
        span, cols = slice(b, b + QB), slice(c, c + chunk)
        back = dot_nt(cotr[span, :], w_down[cols, :])
        grad[span, cols] = (back * slope_ref[span, cols].astype(F32)).astype(BF)

    front(*steps[0])
    for n, (b, c) in enumerate(steps):
        if n + 1 < len(steps):
            front(*steps[n + 1])
        if c + chunk == units:
            span = slice(b, b + QB)
            gn_ref[span, :] = dot_nt(grad[span, :], w_up[...])


def ffn_oth_kernel(meta, n2, cotr, keep, got, gn_ref, low, hid, grad, w_up, w_down):
    for core, (up_ref, down_ref) in enumerate(((keep, got), (got, keep))):

        @pl.when(meta[2] == core)
        def _():
            w_up[...] = up_ref[...]
            w_down[...] = down_ref[...]

    chunk = hid.shape[1] // 2

    def up(c):
        return w_up[:, c * chunk : (c + 1) * chunk]

    def down(c):
        return w_down[:, c * chunk : (c + 1) * chunk]

    feed_forward(n2, cotr, up, down, hid, grad, gn_ref, low)


def output_kernel(meta, low_a, low_b, oth_a, oth_b, mid_ref, out_ref, wide):
    total = mid_ref.shape[0]
    half = total // 2
    for n, (low, oth) in enumerate(((low_a, oth_a), (low_b, oth_b))):
        for b in range(0, half, QB):
            span = slice(b, b + QB)
            rows = slice(n * half + b, n * half + b + QB)
            put_rows(wide, n * half + b, mid_ref[rows, :] + (low[span, :] + oth[span, :]))
    at = total - meta[0] + meta[1] * half
    for b in range(0, half, QB):
        out_ref[b : b + QB, :] = get_rows(wide, at + b, QB).astype(BF)


def ffn_grads_kernel(
    meta, n2_t, cot_t, hid_a, hid_b, grad_a, grad_b, keep_ref, send_ref
):
    half, chunk = hid_a.shape[0], cot_t.shape[0]
    for core in range(2):

        @pl.when(meta[2] == core)
        def _():
            up_ref, down_ref = (keep_ref, send_ref) if core == 0 else (send_ref, keep_ref)
            for c in range(0, hid_a.shape[1], chunk):
                cols = slice(c, c + chunk)
                up_ref[:, cols] = (
                    dot(n2_t[:, :half], grad_a[:, cols])
                    + dot(n2_t[:, half:], grad_b[:, cols])
                ).astype(BF)
                down = dot(cot_t[:, :half], hid_a[:, cols]) + dot(
                    cot_t[:, half:], hid_b[:, cols]
                )
                down_ref[:, cols] = down.T.astype(BF)


def flip_kernel(x_ref, out_ref):
    for b in range(0, x_ref.shape[0], QB):
        out_ref[:, b : b + QB] = x_ref[b : b + QB, :].T


def middle_kernel(
    meta, own_a, own_b, oth_a, oth_b, mid_ref, cotr_a, cotr_b, gain_two,
    gm_ref, gm_own, small_ref,
    wide,
):
    total, width = mid_ref.shape
    half = total // 2
    gain_acc = jnp.zeros((1, width), F32)
    for b in range(0, total, QB):
        span = slice(b, b + QB)
        at = slice(b % half, b % half + QB)
        own = (own_a if b < half else own_b)[at, :]
        mid = mid_ref[span, :]
        e = own + (oth_a if b < half else oth_b)[at, :].astype(F32)
        scale = lax.rsqrt(jnp.mean(mid * mid, axis=-1, keepdims=True) + EPS)
        se = gain_two[...] * e
        mean = jnp.mean(se * mid, axis=-1, keepdims=True)
        grad = (cotr_a if b < half else cotr_b)[at, :].astype(F32) + (
            scale * se - mid * (scale * scale * scale * mean)
        )
        gm_ref[span, :] = grad.astype(BF)
        put_rows(wide, b, grad)
        gain_acc = gain_acc + jnp.sum(own * mid * scale, axis=0, keepdims=True)
    small_ref[...] = jnp.broadcast_to(gain_acc, small_ref.shape)
    back = total - meta[0]
    for b in range(0, half, QB):
        gm_own[b : b + QB, :] = get_rows(wide, back + meta[1] * half + b, QB)


def attn_bwd_kernel(
    band,
    gm, wo_ref, q_ref, k_ref, v_ref, ctx_ref, inv_ref, pl_ref, pt_ref,
    dq_ref, dk_ref, dv_ref, go_ref, ds_ref, sum_ref,
    ds_long, ds_tail, do_ref, kt_ref, dq_t, inner_ref, do_all, dkv_ref,
):
    total, long = gm.shape[0], pl_ref.shape[1]
    index = {pair: n for n, pair in enumerate(band)}
    lane = lax.broadcasted_iota(jnp.int32, (total, 2 * HD), 1)
    do = dot_nt(gm[...], wo_ref[...]).astype(BF).astype(F32) * inv_ref[...]
    do = do.astype(BF)
    k_t = k_ref[...].T
    inner_t = (do.astype(F32) * ctx_ref[...].astype(F32)).T
    inner = []
    extra = kt_ref.shape[1] - HD
    marks = lax.broadcasted_iota(jnp.int32, (extra, total), 0)
    marks = marks == lax.broadcasted_iota(jnp.int32, (extra, total), 1) // BLK
    marks = jnp.where(marks, 1.0, 0.0).astype(BF)
    for hh in range(2):
        do_ref[hh] = jnp.where((lane < HD) == (hh == 0), do, jnp.zeros_like(do))
        kt_ref[hh, 0:HD, :] = k_t[hh * HD : (hh + 1) * HD, :]
        kt_ref[hh, HD:, :] = marks
        inner.append(jnp.sum(inner_t[hh * HD : (hh + 1) * HD, :], axis=0, keepdims=True))
    inner_ref[...] = jnp.concatenate(
        [jnp.broadcast_to(rows, (8, total)) for rows in inner], axis=0
    )

    def head(hh, carry):
        rows_of_head = pl.ds(pl.multiple_of(hh * HD, HD), HD)
        row = inner_ref[pl.ds(pl.multiple_of(hh * 8, 8), 8), :][0:1, :]
        for start in range(0, total, QB):
            lo, hi = (0, long) if start < long else (long, total)
            terms, ds_here = (pl_ref, ds_long) if start < long else (pt_ref, ds_tail)
            cols = slice(start - lo, start - lo + QB)
            for j in range(lo, hi, BLK):
                rows = slice(j - lo, j - lo + BLK)
                dp = dot_nt(v_ref[j : j + BLK, :], do_ref[hh, start : start + QB, :])
                ds = terms[hh, rows, cols].astype(F32) * (dp - row[:, start : start + QB])
                ds = ds.astype(BF)
                ds_here[rows, cols] = ds
                for c in range(0, QB, BLK):
                    pair = (j // BLK, (start + c) // BLK)
                    if pair in index:
                        ds_ref[hh, index[pair]] = ds[:, c : c + BLK]
            sums = dot(kt_ref[hh, :, lo:hi], ds_here[:, cols])
            dq_t[rows_of_head, start : start + QB] = sums[0:HD, :]
            sum_ref[hh, :, start : start + QB] = sums[HD:, :]
        for lo, hi, ds_here, terms in (
            (0, long, ds_long, pl_ref), (long, total, ds_tail, pt_ref)
        ):
            dkv_ref[hh, 0, lo:hi, :] = dot(ds_here[...], q_ref[lo:hi, :])
            dkv_ref[hh, 1, lo:hi, :] = dot(terms[hh], do_all[lo:hi, :])
        return carry

    do_all[...] = do
    lax.fori_loop(0, 2, head, 0)
    dq = dq_t[...].T * HD ** (-0.5)
    dk = jnp.where(lane < HD, dkv_ref[0, 0], dkv_ref[1, 0])
    dv = jnp.where(lane < HD, dkv_ref[0, 1], dkv_ref[1, 1])
    dq_ref[...] = dq.astype(BF)
    dk_ref[...] = dk.astype(BF)
    dv_ref[...] = dv.astype(BF)
    go_ref[...] = dot(ctx_ref[...].T, gm[...]).astype(BF)


def grads_kernel(pairs, meta, nx_t, *refs):
    pieces, go_pieces = refs[: 3 * pairs], refs[3 * pairs : 4 * pairs]
    keep_ref, send_ref, dqkv = refs[4 * pairs :]
    rows, local = keep_ref.shape[0], pairs * 2 * HD
    for n, piece in enumerate(pieces):
        dqkv[:, n * BLK : (n + 1) * BLK] = piece[...]
    for core in range(2):

        @pl.when(meta[2] == core)
        def _():
            for out, part in ((send_ref, 1 - core), (keep_ref, core)):
                grad = dot(nx_t[part * rows : (part + 1) * rows, :], dqkv[...])
                out[:, : 3 * local] = grad.astype(BF)
                for n, piece in enumerate(go_pieces):
                    out[n * BLK : (n + 1) * BLK, 3 * local :] = piece[
                        :, part * rows : (part + 1) * rows
                    ]


def normed_kernel(pairs, meta, xr_ref, dqkv, wq, wk, wv, gn_own, gn_send, small_ref, wide):
    total, width = xr_ref.shape
    half, local = total // 2, pairs * 2 * HD
    gain_acc = jnp.zeros((1, width), F32)
    for b in range(0, total, QB):
        span = slice(b, b + QB)
        back = sum(
            dot_nt(dqkv[span, n * local : (n + 1) * local], w[...])
            for n, w in enumerate((wq, wk, wv))
        )
        x = xr_ref[span, :].astype(F32)
        scale = lax.rsqrt(jnp.mean(x * x, axis=-1, keepdims=True) + EPS)
        gain_acc = gain_acc + jnp.sum(back * x * scale, axis=0, keepdims=True)
        put_rows(wide, b, back)
    small_ref[...] = jnp.broadcast_to(gain_acc, small_ref.shape)
    at = total - meta[0]
    for b in range(0, half, QB):
        gn_own[b : b + QB, :] = get_rows(wide, at + meta[1] * half + b, QB)
        gn_send[b : b + QB, :] = get_rows(
            wide, at + (1 - meta[1]) * half + b, QB
        ).astype(BF)


def table_kernel(diagonal, blocks, bkt_ref, ds_ref, sum_ref, out_ref):
    lane = lax.broadcasted_iota(jnp.int32, (8, BLK), 1)
    levels, tiles = BUCKETS // 2, BLK // 8
    beside = (ds_ref.shape[1] - diagonal) // 2

    def counted(wanted, n, hh, sums):
        cells = ds_ref[hh, n].astype(F32).reshape(tiles, 8, BLK)
        bucket = bkt_ref[n].reshape(tiles, 8, BLK)
        return tuple(
            total
            + jnp.sum(jnp.where(bucket[r0:r1] == b, cells[r0:r1], 0.0), axis=0)
            for total, (b, r0, r1) in zip(sums, wanted)
        )

    reach = [b if b < levels // 2 else LIMITS[b - levels // 2] - 1 for b in range(levels - 1)]
    spans = [sum(8 * r + 1 <= n for r in range(tiles)) for n in reach[1:]] + [tiles]
    parts = (
        (0, diagonal, [(b, 0, tiles) for b in range(BUCKETS) if b != levels]),
        (diagonal, beside, [(levels + 1 + n, 0, s) for n, s in enumerate(spans)]),
        (diagonal + beside, beside, [(1 + n, tiles - s, tiles) for n, s in enumerate(spans)]),
    )
    zero = jnp.zeros((8, BLK), F32)

    def head(hh, carry):
        sums = [zero] * BUCKETS
        for first, count, wanted in parts:
            found = lax.fori_loop(
                first,
                first + count,
                lambda n, part, wanted=wanted: counted(wanted, n, hh, part),
                (zero,) * len(wanted),
            )
            for (b, _, _), part in zip(wanted, found):
                sums[b] = sums[b] + part
        for i in range(blocks):
            cols = sum_ref[hh, 0:8, i * BLK : (i + 1) * BLK]
            key_block = lax.broadcasted_iota(jnp.int32, (8, BLK), 0)
            far = (key_block < blocks) & (jnp.abs(key_block - i) > 1)
            for b, side in ((levels - 1, key_block < i), (BUCKETS - 1, key_block > i)):
                sums[b] = sums[b] + jnp.where(far & side, cols, 0.0)
        row = zero
        for b in range(BUCKETS):
            row = jnp.where(lane == b, jnp.sum(sums[b]), row)
        out_ref[hh] = row
        return carry

    lax.fori_loop(0, 2, head, 0)


def final_kernel(
    x_ref, gain, gn_own, gn_oth, gm_ref, grad_ref
):
    for b in range(0, x_ref.shape[0], QB):
        span = slice(b, b + QB)
        x = x_ref[span, :].astype(F32)
        e = gn_own[span, :] + gn_oth[span, :].astype(F32)
        scale = lax.rsqrt(jnp.mean(x * x, axis=-1, keepdims=True) + EPS)
        se = gain[...] * e
        mean = jnp.mean(se * x, axis=-1, keepdims=True)
        grad_ref[span, :] = (
            gm_ref[span, :] + (scale * se - x * (scale * scale * scale * mean))
        ).astype(BF)


def add_kernel(at, meta, keep, got, *outs):
    rows = outs[0].shape[0]
    if len(outs) == 1:
        outs[0][...] = (keep[...].astype(F32) + got[...].astype(F32)).astype(BF)
        return
    for out, part in ((outs[0], meta[at]), (outs[1], 1 - meta[at])):
        span = pl.ds(pl.multiple_of(part * rows, 16), rows)
        out[...] = (keep[span, :].astype(F32) + got[span, :].astype(F32)).astype(BF)


def join_kernel(at, meta, mine, *refs):
    got, out = refs[:-1], refs[-1]
    rows, cut = mine.shape[0], got[0].shape[1]
    out[pl.ds(pl.multiple_of(meta[at] * rows, 16), rows), :] = mine[...]
    there = pl.ds(pl.multiple_of((1 - meta[at]) * rows, 16), rows)
    for n, part in enumerate(got):
        out[there, n * cut : (n + 1) * cut] = part[...]


def little_kernel(a_ref, b_ref, out_ref):
    out_ref[...] = a_ref[...] + b_ref[...]


def split_ffn_kernel(meta, mine, got, up_ref, down_ref):
    width = down_ref.shape[1]
    for core in range(2):

        @pl.when(meta[2] == core)
        def _():
            up, down = (mine, got) if core == 0 else (got, mine)
            up_ref[...] = up[...].astype(F32)
            for n in range(down.shape[1] // width):
                rows = slice(n * down.shape[0], (n + 1) * down.shape[0])
                down_ref[rows, :] = down[:, n * width : (n + 1) * width].astype(F32)


def split_attn_kernel(meta, mine, got, q_ref, k_ref, v_ref, o_ref):
    rows, local = mine.shape[0], q_ref.shape[1]
    for core in range(2):

        @pl.when(meta[2] == core)
        def _():
            for n, part in enumerate((mine, got) if core == 0 else (got, mine)):
                span = slice(n * rows, (n + 1) * rows)
                for m, out in enumerate((q_ref, k_ref, v_ref)):
                    out[span, :] = part[:, m * local : (m + 1) * local].astype(F32)
                o_ref[:, span] = part[:, 3 * local :].astype(F32)


def swap(value, size, flip, axis="dp"):
    return lax.ppermute(value, axis, [(n, flip(n)) for n in range(size)])


class Exchange:
    def __init__(self, name, meta, size, orders):
        self.name, self.meta, self.size, self.orders = name, meta, size, orders
        self.phase, self.joins, self.waiting = -1, [], -2

    def gather(self, piece, cuts):
        self.keep, self.joins = piece, list(range(cuts))
        self.back()
        return self

    def sum(self, keep, send):
        self.keep = keep
        self.got = swap(send, self.size, lambda n: n ^ 1)
        return self

    def flip(self, phase):
        if phase < 0:
            return lambda n: n ^ 1
        orders = self.orders
        return lambda n: n ^ (1 << orders[n & 1][phase])

    def pair(self, value):
        return (value, full(value.shape))

    def reduce(self, after=()):
        self.phase += 1
        shape = self.keep.shape
        last = self.phase == len(self.orders[0])
        cut = not last and shape[0] % 32 == 0
        rows = shape[0] // 2 if cut else shape[0]
        out = (jax.ShapeDtypeStruct((rows, shape[1]), BF), full((rows, shape[1])))
        parts = call(
            functools.partial(add_kernel, 3 + self.phase),
            [(self.meta, smem()), self.pair(self.keep), self.pair(self.got)],
            [out, out] if cut else [out],
            name=f"{self.name}_add{self.phase}",
            after=after,
        )
        self.keep = parts[0]
        if last:
            self.back()
            return self.keep
        if cut:
            self.joins.append(self.phase)
        self.got = swap(parts[-1], self.size, self.flip(self.phase))
        return self.keep

    def back(self, parts=1):
        phase = self.joins.pop() if self.joins else -1
        self.waiting = phase
        if parts > 1:
            self.got = [
                swap(v, self.size, self.flip(phase))
                for v in jnp.split(self.keep, parts, axis=1)
            ]
            return
        self.got = swap(self.keep, self.size, self.flip(phase))

    def join(self, after=(), parts=1):
        rows, cols = self.keep.shape
        got = self.got if isinstance(self.got, list) else [self.got]
        self.keep = call(
            functools.partial(join_kernel, 3 + self.waiting),
            [(self.meta, smem()), self.pair(self.keep)] + [self.pair(v) for v in got],
            [(jax.ShapeDtypeStruct((2 * rows, cols), BF), full((2 * rows, cols)))],
            name=f"{self.name}_join{self.waiting}",
            after=after,
        )[0]
        self.back(parts)
        return self.keep


def body(
    inputs, norm_one, w_query, w_key, w_value, w_out, bias_table, norm_two, w_up, w_down,
    doc_lengths, layout_steps, cotangent, *, size,
):
    row_len = layout_steps.shape[0]
    half, width = inputs.shape
    long = 3 * row_len // 4
    local = w_query.shape[1]
    pairs = local // (2 * HD)
    hidden_units = w_up.shape[1]
    mp = lax.axis_index("mp")
    dp = lax.axis_index("dp")
    core = dp & 1
    band = band_blocks(long // BLK, row_len // BLK)
    count = len(band)

    def other(value):
        return swap(value, 2, lambda n: 1 - n, "mp")

    def core_swap(value):
        return swap(value, size, lambda n: n ^ 1)

    doc_ends = jnp.cumsum(doc_lengths[0])
    turn = jnp.sum(
        jnp.where(doc_lengths[0] == long, doc_ends - doc_lengths[0], 0)
    ).astype(jnp.int32)
    places = jnp.arange(row_len, dtype=jnp.int32)
    segment = jnp.sum((places[:, None] >= doc_ends[None, :]).astype(jnp.int32), axis=1)
    position = jnp.cumsum(layout_steps)
    both = jnp.stack([position, segment])
    both = lax.dynamic_slice_in_dim(
        jnp.concatenate([both, both], axis=1), turn, row_len, 1
    ).astype(jnp.int32)

    table = jnp.pad(bias_table.T, ((0, 8 - bias_table.shape[1]), (0, 0)))
    table = jnp.concatenate(
        [table, jnp.full((8, BLK - BUCKETS), MASKED, F32)], axis=1
    )
    gain_one, gain_two = norm_one.reshape(1, width), norm_two.reshape(1, width)

    depth = size.bit_length() - 1
    rest = list(range(1, depth))
    orders = (rest, rest[1:] + rest[:1])
    bits = [(dp >> b) & 1 for b in range(depth)]
    phase_bits = [
        jnp.where(core == 0, bits[orders[0][t]], bits[orders[1][t]])
        for t in range(depth - 1)
    ]
    meta = jnp.stack([turn, mp, core] + phase_bits).astype(jnp.int32)

    shape = jax.ShapeDtypeStruct
    heads = 2 * pairs
    tail = row_len - long
    part = width // 2
    pair_block = pl.BlockSpec((row_len, 2 * HD), lambda p: (0, p))
    weight_block = pl.BlockSpec((width, 2 * HD), lambda p: (0, p))

    def whole(value):
        return (value, full(value.shape))

    def out(dims, kind=BF, spec=None):
        return (shape(dims, kind), spec or full(dims))

    def cuts_of(rows):
        cuts = 0
        while cuts < depth - 1 and rows % 32 == 0:
            rows, cuts = rows // 2, cuts + 1
        return cuts, rows

    def piece_of(rows):
        cuts, least = cuts_of(rows)
        return sum(phase_bits[t] * (rows // least >> (t + 1)) for t in range(cuts))

    ffn_cuts, ffn_rows = cuts_of(width)
    at = jnp.stack([piece_of(width), core]).astype(jnp.int32)
    anywhere = pl.BlockSpec(memory_space=pl.ANY)
    x_oth = other(inputs)
    early = 3 * half // 8
    ffn_piece, wo_send, cot_a = call(
        pieces_kernel,
        [
            (at, smem()), (w_out, anywhere), (w_up, anywhere), (w_down, anywhere),
            (cotangent, anywhere),
        ],
        [out((ffn_rows, hidden_units)), out((local, part)), out((early, width))],
        name="pieces",
        scratch=[pltpu.SemaphoreType.DMA((4,))],
        limit=VMEM_LIMIT,
        after=[both, meta, table, gain_one, gain_two],
    )
    ffn_piece = other(ffn_piece)
    wo_a = other(wo_send)
    cot_a = other(cot_a)

    work = [
        pltpu.VMEM((2, long, QB), F32),
        pltpu.VMEM((2, HD + 16, row_len), BF),
        pltpu.VMEM((2, row_len, 2 * HD), BF),
        pltpu.VMEM((row_len, 2 * HD), BF),
        pltpu.VMEM((2 * HD, row_len), F32),
    ]
    wide = pltpu.VMEM((width // BLK, 2 * row_len, BLK), F32)
    long_spec = pl.BlockSpec((2, long, long), lambda p: (p, 0, 0))
    tail_spec = pl.BlockSpec((2, tail, tail), lambda p: (p, 0, 0))
    xr, nx, qs, keys, values, ctx_own, inv, p_long, p_tail, bkt = call(
        functools.partial(attn_own_kernel, long, band),
        [
            (meta, smem()), whole(inputs), whole(x_oth), whole(gain_one), whole(both),
            (w_query, weight_block), (w_key, weight_block), (w_value, weight_block),
            whole(table),
        ],
        [
            out((row_len, width)), out((row_len, width)),
            out((row_len, local), BF, pair_block), out((row_len, local), BF, pair_block),
            out((row_len, local), BF, pair_block), out((row_len, local), BF, pair_block),
            out((row_len, local), F32, pair_block), out((heads, long, long), BF, long_spec),
            out((heads, tail, tail), BF, tail_spec), out((count, BLK, BLK), jnp.int32),
        ],
        name="attend_own",
        grid=(pairs,),
        scratch=[wide] + work + [pltpu.VMEM((2 * HD, row_len), F32)],
    )

    ctx_send, ffn_piece, wo_a, cot_a = call(
        copy_kernel,
        [whole(v) for v in (ctx_own, ffn_piece, wo_a, cot_a)],
        [out(v.shape) for v in (ctx_own, ffn_piece, wo_a, cot_a)],
        name="take_pieces",
    )
    ctx_oth = other(ctx_send)
    (cot_send,) = call(
        copy_kernel, [whole(cotangent[early:])], [out((half - early, width))],
        name="take_cotangent", after=[ctx_send],
    )
    cot_b = other(cot_send)
    ffn_w = Exchange("ffn_w", meta, size, orders).gather(ffn_piece, ffn_cuts)
    wo_b = core_swap(wo_a)
    mark = wo_b
    if ffn_w.waiting >= 0:
        mark = ffn_w.join([wo_b])

    mid, n2_a, n2_b, n2_t = call(
        join_heads_kernel,
        [
            (meta, smem()), whole(xr), whole(ctx_own), whole(ctx_oth), whole(w_out),
            whole(wo_a), whole(wo_b), whole(gain_two),
        ],
        [
            out((row_len, width), F32), out((half, width)), out((half, width)),
            out((width, row_len)),
        ],
        name="join_heads",
        after=[mark],
    )
    n2 = (n2_a, n2_b)
    mark = n2_b
    hid, slopes, low = [], [], []
    for h in range(2):
        hid_h, slope_h, low_h = call(
            feed_kernel,
            [whole(n2[h]), whole(w_up), whole(w_down)],
            [out((half, hidden_units)), out((half, hidden_units)), out((half, width), F32)],
            name=f"feed{h}",
            after=[mark],
        )
        mark = low_h
        hid.append(hid_h)
        slopes.append(slope_h)
        low.append(low_h)
    *cotr, cot_t = call(
        turn_kernel,
        [(meta, smem()), whole(cotangent), whole(cot_a), whole(cot_b)],
        [out((half, width)), out((half, width)), out((width, row_len))],
        name="turn_cotangent",
        scratch=[wide],
        after=[mark],
    )
    mark = cot_t
    if ffn_w.waiting >= 0 and ffn_w.joins:
        mark = ffn_w.join([mark])
    grad_pre, gn2_own, gn2_oth, low_oth = [], [], [], []
    for h in range(2):
        grad_h, own_h = call(
            feed_back_kernel,
            [whole(cotr[h]), whole(slopes[h]), whole(w_up), whole(w_down)],
            [out((half, hidden_units)), out((half, width), F32)],
            name=f"feed_back{h}",
            after=[mark],
        )
        mark = own_h
        grad_pre.append(grad_h)
        gn2_own.append(own_h)
    ffn_keep, ffn_send = call(
        ffn_grads_kernel,
        [(meta, smem()), whole(n2_t), whole(cot_t)] + [whole(v) for v in hid + grad_pre],
        [out((width, hidden_units)), out((width, hidden_units))],
        name="ffn_grads",
        after=[mark],
    )
    ffn = Exchange("ffn", meta, size, orders).sum(ffn_keep, ffn_send)
    mark = ffn_keep
    while ffn_w.waiting >= 0:
        mark = ffn_w.join([mark])
    mark = ffn.reduce([mark])
    for h in range(2):
        oth_h, low_h = call(
            ffn_oth_kernel,
            [
                (meta, smem()), whole(n2[h]), whole(cotr[h]), whole(ffn_w.keep),
                whole(ffn_w.got),
            ],
            [out((half, width), F32), out((half, width), F32)],
            name=f"feed_oth{h}",
            scratch=[
                pltpu.VMEM((half, hidden_units), BF),
                pltpu.VMEM((half, hidden_units), BF),
                pltpu.VMEM((width, hidden_units), BF),
                pltpu.VMEM((width, hidden_units), BF),
            ],
            after=[mark],
        )
        mark = low_h
        gn2_oth.append(oth_h)
        low_oth.append(low_h)
    mark = mark_one = ffn.reduce([mark])
    (nx_t,) = call(
        flip_kernel, [whole(nx)], [out((width, row_len))], name="flip", after=[mark]
    )

    gm, gm_own, small_two = call(
        middle_kernel,
        [(meta, smem())]
        + [whole(v) for v in gn2_own + gn2_oth]
        + [whole(mid)]
        + [whole(v) for v in cotr]
        + [whole(gain_two)],
        [out((row_len, width)), out((half, width), F32), out((8, width), F32)],
        name="grad_middle",
        scratch=[wide],
        after=[nx_t],
    )
    tables = []

    def table_sums(p, after):
        (sums,) = call(
            functools.partial(table_kernel, row_len // BLK, long // BLK),
            [whole(bkt), whole(ds_pieces[p]), whole(sum_pieces[p])],
            [out((2, 8, BLK), F32)],
            name=f"table_sums{p}",
            after=after,
        )
        tables.append(sums)
        return sums

    pieces, go_pieces, ds_pieces, sum_pieces = [], [], [], []
    for p in range(pairs):
        pair = pl.BlockSpec((row_len, 2 * HD), lambda *_, p=p: (0, p))
        dq, dk, dv, go, ds, sums = call(
            functools.partial(attn_bwd_kernel, band),
            [
                whole(gm), (w_out, pl.BlockSpec((2 * HD, width), lambda *_, p=p: (p, 0))),
                (qs, pair), (keys, pair), (values, pair), (ctx_own, pair), (inv, pair),
                (p_long, pl.BlockSpec((2, long, long), lambda *_, p=p: (p, 0, 0))),
                (p_tail, pl.BlockSpec((2, tail, tail), lambda *_, p=p: (p, 0, 0))),
            ],
            [
                out((row_len, 2 * HD)), out((row_len, 2 * HD)), out((row_len, 2 * HD)),
                out((2 * HD, width)), out((2, count, BLK, BLK)), out((2, 16, row_len), F32),
            ],
            name=f"attend_back{p}",
            scratch=[
                pltpu.VMEM((long, long), BF),
                pltpu.VMEM((tail, tail), BF),
                pltpu.VMEM((2, row_len, 2 * HD), BF),
                pltpu.VMEM((2, HD + 16, row_len), BF),
                pltpu.VMEM((2 * HD, row_len), F32),
                pltpu.VMEM((16, row_len), F32),
                pltpu.VMEM((row_len, 2 * HD), BF),
                pltpu.VMEM((2, 2, row_len, 2 * HD), F32),
            ],
            after=[mark],
        )
        pieces.append((dq, dk, dv))
        go_pieces.append(go)
        ds_pieces.append(ds)
        sum_pieces.append(sums)
        mark = dq
        if p == 1:
            for _ in range(depth - 3):
                mark = ffn.reduce([mark])
    mark = table_sums(0, [mark])
    mark = ffn.reduce([mark])
    operands = [whole(pieces[p][n]) for n in range(3) for p in range(pairs)]
    attn_keep, attn_send, dqkv = call(
        functools.partial(grads_kernel, pairs),
        [(meta, smem()), whole(nx_t)] + operands + [whole(go) for go in go_pieces],
        [
            out((part, 3 * local + part)), out((part, 3 * local + part)),
            out((row_len, 3 * local)),
        ],
        name="attend_grads",
        after=[mark],
    )
    attn = Exchange("attn", meta, size, orders).sum(attn_keep, attn_send)
    gn_own, gn_send, small_one = call(
        functools.partial(normed_kernel, pairs),
        [
            (meta, smem()), whole(xr), whole(dqkv), whole(w_query), whole(w_key),
            whole(w_value),
        ],
        [out((half, width), F32), out((half, width)), out((8, width), F32)],
        name="grad_normed",
        scratch=[wide],
    )
    gn_oth = other(gn_send)
    gains = jnp.concatenate([small_one[0:1], small_two[0:1]], axis=0)
    gains = gains.reshape(2 * width // BLK, BLK)
    gains_oth = other(gains)

    def join_ffn(after, parts=1):
        return ffn.join([after], parts) if ffn.waiting >= 0 and ffn.joins else after

    mark = attn.reduce([small_one])
    mark = table_sums(1, [mark])
    mark = attn.reduce([mark])
    mark = join_ffn(mark, 2)
    for p in range(2, pairs):
        mark = table_sums(p, [mark])
    little = jnp.concatenate([gains + gains_oth] + [t[:, 0, :] for t in tables], axis=0)
    got, phase = swap(little, size, attn.flip(0)), 0

    def little_step(after):
        nonlocal little, got, phase
        little = call(
            little_kernel,
            [whole(little), whole(got)],
            [out(little.shape, F32)],
            name=f"little{phase}",
            after=[after],
        )[0]
        phase += 1
        if phase < depth:
            got = swap(little, size, attn.flip(phase if phase < depth - 1 else -1))
        return little

    while attn.phase < depth - 2:
        mark = attn.reduce([mark, gains_oth])
    mark = little_step(mark)
    mark = attn.reduce([mark, gn_oth])
    mark = little_step(mark)
    mark = join_ffn(mark)
    mark = attn.join([mark]) if attn.waiting >= 0 else mark
    (output,) = call(
        output_kernel,
        [(meta, smem())] + [whole(v) for v in low + low_oth] + [whole(mid)],
        [out((half, width))],
        name="output",
        scratch=[wide],
        limit=VMEM_LIMIT,
        after=[mark],
    )
    mark = output
    while phase < depth - 1:
        mark = little_step(mark)
    while attn.waiting > 0:
        mark = attn.join([mark])
    while ffn.waiting >= 0:
        mark = ffn.join([mark])
    (input_grad,) = call(
        final_kernel,
        [
            whole(inputs), whole(gain_one), whole(gn_own), whole(gn_oth), whole(gm_own),
        ],
        [out((half, width))],
        name="input_grad",
        after=[mark],
    )
    grad_up, grad_down = call(
        split_ffn_kernel,
        [(meta, smem()), whole(ffn.keep), whole(ffn.got)],
        [out((width, hidden_units), F32), out((hidden_units, width), F32)],
        name="ffn_split",
        after=[input_grad],
    )
    mark = grad_up
    if attn.waiting >= 0:
        mark = attn.join([mark])
    little_step(mark)
    grad_query, grad_key, grad_value, grad_out = call(
        split_attn_kernel,
        [(meta, smem()), whole(attn.keep), whole(attn.got)],
        [
            out((width, local), F32), out((width, local), F32), out((width, local), F32),
            out((local, width), F32),
        ],
        name="attn_split",
    )
    gains = little[: 2 * width // BLK].reshape(2, width)
    grad_table = little[2 * width // BLK :, :BUCKETS].T
    return (
        output, input_grad, gains[0], gains[1], grad_query, grad_key, grad_value,
        grad_out, grad_table, grad_up, grad_down,
    )


def solution(mesh):
    placed = (
        P(("dp", "mp"), None),
        P(),
        P(None, "mp"),
        P(None, "mp"),
        P(None, "mp"),
        P("mp", None),
        P(None, "mp"),
        P(),
        P(None, "mp"),
        P("mp", None),
        P("dp", None),
        P("dp"),
        P(("dp", "mp"), None),
    )
    return jax.shard_map(
        functools.partial(body, size=mesh.shape["dp"]),
        mesh=mesh,
        in_specs=placed,
        out_specs=(
            P(("dp", "mp"), None),
            P(("dp", "mp"), None),
            P(),
            P(),
            P(None, "mp"),
            P(None, "mp"),
            P(None, "mp"),
            P("mp", None),
            P(None, "mp"),
            P(None, "mp"),
            P("mp", None),
        ),
        check_vma=False,
    )
```
